32 devices in a mesh: groups: 2 (over x), expert: 16 (over z, y, core).
Axes of the slice: x: 2, y: 2, z: 4, core: 2. Of those that a mesh axis runs over, the one named last changes fastest.
Arguments:
- tokens: bfloat16 [4096, 2048], P(('groups', 'expert')), parts along dimension 0, may hold values from -12 to 12
- out_grad: bfloat16 [4096, 2048], P(('groups', 'expert')), parts along dimension 0, may hold values from -6 to 6
- cluster_ids: int32 [4096], P(('groups', 'expert')), parts along dimension 0, may hold values from 0 to 31, as said below
- routes: int32 [1024, 8], P(('groups', 'expert')), parts along dimension 0, may hold values from 0 to 15, all different within a row; in each aligned block of 32 rows (0 to 31, 32 to 63, ...) at most 32 rows name the same one
- route_weights: float32 [1024, 8], P(('groups', 'expert')), parts along dimension 0, may hold values from 0.05 to 0.5
- gate_weight: bfloat16 [16, 2048, 768], P('expert'), may hold values from -0.125 to 0.125
- up_weight: bfloat16 [16, 2048, 768], P('expert'), may hold values from -0.125 to 0.125
- down_weight: bfloat16 [16, 768, 2048], P('expert'), may hold values from -0.21875 to 0.21875
Outputs:
- layer_out: float32 [4096, 2048], P(('groups', 'expert')), parts along dimension 0
- token_grad: float32 [4096, 2048], P(('groups', 'expert')), parts along dimension 0
The draws below stay inside these ranges and needn't reach their ends.
There are 2 independent parts, one for each index of `groups`. The reference program is written for one: setup_inputs(seed, part) draws one part's arguments, and reference() takes and returns one part's arrays. A program takes and returns all parts, laid end to end along the dimension named above; an argument that names none is the same for every part. Nothing has to cross between parts.
Inputs may be any that keep to these rules, and one draw needn't show every extreme that they name: `cluster_ids`: within each block of 128 tokens every one of the 32 cluster numbers occurs at least once. `routes`: each row names 8 different experts. Among the 32 rows of one index of expert no expert is named more than 32 times, and in some such blocks one expert is named exactly 32 times.
All inputs are finite; a program needn't handle non-finite values.
Results may differ from the reference program's by a relative error of at most 0.0027.
Values may be sent and summed in bfloat16 or wider, within the bound.
A program may use at most 64 MiB of HBM per device.

```python
import math
import jax
import jax.numpy as jnp
import numpy as np
from jax import lax

D = 2048
FF = 768
TOP = 8
CENT_DEV = 32
TOK_DEV = 128
EXPERTS = 16
TOKENS = 2048
CENTROIDS = 512
CAP = 32
N_EXPERT = 16


def draw_cluster_ids(key, part):
    blocks = TOKENS // TOK_DEV
    key_fill = jax.random.fold_in(key, 11)
    key_order = jax.random.fold_in(key, 23)
    extra = jax.random.randint(key_fill, (blocks, TOK_DEV - CENT_DEV), 0, CENT_DEV, dtype=jnp.int32)
    every_one = jnp.broadcast_to(jnp.arange(CENT_DEV, dtype=jnp.int32)[None, :], (blocks, CENT_DEV))
    joined = jnp.concatenate([every_one, extra], axis=1)
    order_keys = jax.random.split(key_order, blocks)
    shuffled = jax.vmap(lambda one_key, one_row: jax.random.permutation(one_key, one_row))(order_keys, joined)
    return shuffled.reshape(TOKENS).astype(jnp.int32)


def steps_of(stream_key, shape, pieces, least, top_value):
    factor_of = 1.0
    for dim, blocks in pieces:
        heights = jax.random.uniform(jax.random.fold_in(jax.random.fold_in(stream_key, 6), dim), (blocks,), jnp.float32, least / len(pieces), top_value / len(pieces))
        factor_of = factor_of * jnp.repeat(jnp.exp(heights), shape[dim] // blocks).reshape((-1,) + (1,) * (len(shape) - 1 - dim))
    return factor_of


def assign_block(key, own, number, rows, amount, top, bound, slope):
    ranking = jax.random.permutation(key, amount)
    packed, ordinary = portions_of(amount, rows * top, bound, slope, True), portions_of(amount, rows * top, bound, slope, False)
    places = jnp.arange(amount)

    def named(lengths, turn):
        used = int((lengths > 0).sum())
        fixed = max(1, used // 4)
        shifted = fixed + (places - fixed + turn * (used - fixed)) % max(1, amount - fixed)
        return jnp.zeros((amount,), jnp.int32).at[ranking[jnp.where(places < fixed, places, shifted)]].set(jnp.asarray(lengths, jnp.int32))

    lengths = jnp.where(number % 4 == 0, named(packed, number // 4), named(ordinary, number - number // 4 - 1))
    mixed = jax.random.permutation(jax.random.fold_in(own, 3), amount)
    giver, taker = mixed[0:amount // 2 * 2:2], mixed[1:amount // 2 * 2:2]
    margin = jnp.minimum(lengths[giver] - 1, bound - lengths[taker]) // 2
    margin = jnp.where((giver == ranking[0]) | (taker == ranking[0]) | (lengths[taker] == 0), 0, jnp.maximum(margin, 0))
    shifted = jax.random.randint(jax.random.fold_in(own, 4), (amount // 2,), 0, 1 << 20) % (margin + 1)
    lengths = lengths.at[giver].add(-shifted).at[taker].add(shifted)
    items = jnp.searchsorted(jnp.cumsum(lengths), jnp.arange(rows * top), side="right").astype(jnp.int32)
    table = items.reshape(top, rows).T
    table = table[jax.random.permutation(jax.random.fold_in(own, 1), rows)]
    turn = jax.random.randint(jax.random.fold_in(own, 2), (rows, 1), 0, top)
    return jnp.take_along_axis(table, (jnp.arange(top)[None, :] + turn) % top, axis=1)


def portions_of(count, total, most, slope, full):
    weights = [(1 << 20) // math.isqrt(standing ** slope) + 1 for standing in range(1, count + 1)]
    largest = most if full else min(most, max(-(-total // count), total * weights[0] // sum(weights)))
    least = 1 if total - largest >= count - 1 else 0
    holding, spare = [largest] + [least] * (count - 1), total - largest - least * (count - 1)
    while spare > 0:
        candidates = [i for i in range(1, count) if holding[i] < largest] or [i for i in range(1, count) if holding[i] < most]
        pool, remaining = sum([weights[i] for i in candidates]), spare
        for i in candidates:
            addition = min(most - holding[i], max(1, remaining * weights[i] // pool), spare)
            holding[i] = holding[i] + addition
            spare = spare - addition
    return np.array(holding)


def centred(rng, extent, deviation, most, cuts=(), kind=jnp.bfloat16):
    factor_of = steps_of(rng, extent, cuts, -0.22, 0.18) if cuts else 1.0
    entries = jax.random.normal(rng, extent, jnp.float32) * deviation * factor_of
    return jnp.minimum(jnp.maximum(entries, -most), most).astype(kind)


def setup_inputs(seed: int = 0, part: int = 0) -> dict:
    key_of = jax.random.split(jax.random.key(seed), 9)
    part_keys = jax.random.split(jax.random.fold_in(key_of[8], part), 9)
    tokens = centred(part_keys[0], (TOKENS, D), 2.0, 12.0, ((0, 16),))
    out_grad = centred(part_keys[1], (TOKENS, D), 1.0, 6.0, ((0, 16),))
    cluster_ids = draw_cluster_ids(jax.random.fold_in(jax.random.fold_in(key_of[8], part), 71), part)
    routes_keys = jax.random.split(jax.random.fold_in(part_keys[3], 1), CENTROIDS // CENT_DEV)
    routes_turns = jax.random.permutation(jax.random.fold_in(part_keys[3], 3), CENTROIDS // CENT_DEV)
    routes = jax.vmap(lambda own, number: assign_block(jax.random.fold_in(part_keys[3], 2), own, number, CENT_DEV, EXPERTS, TOP, CAP, 2))(routes_keys, routes_turns).reshape((CENTROIDS, TOP))
    route_weights = jnp.clip(jnp.exp(math.log(0.5) - 2.3025851 * jax.random.uniform(part_keys[4], (CENTROIDS, TOP), jnp.float32) ** steps_of(part_keys[4], (CENTROIDS, TOP), ((0, 16),), -0.2, 0.2)), 0.05, 0.5)
    gate_weight = centred(key_of[5], (EXPERTS, D, FF), D ** -0.5, 0.125, ((0, 16),))
    up_weight = centred(key_of[6], (EXPERTS, D, FF), D ** -0.5, 0.125, ((0, 16),))
    down_weight = centred(key_of[7], (EXPERTS, FF, D), FF ** -0.5, 0.21875, ((0, 16),))
    return {"tokens": tokens, "out_grad": out_grad, "cluster_ids": cluster_ids, "routes": routes, "route_weights": route_weights, "gate_weight": gate_weight, "up_weight": up_weight, "down_weight": down_weight}


def reference(tokens, out_grad, cluster_ids, routes, route_weights, gate_weight, up_weight, down_weight):
    blocks = N_EXPERT
    pair_count = CENT_DEV * TOP
    tok_blocks = tokens.reshape(blocks, TOK_DEV, D)
    grad_blocks = out_grad.reshape(blocks, TOK_DEV, D)
    cluster_blocks = cluster_ids.reshape(blocks, TOK_DEV)
    member = (cluster_blocks[:, :, None] == jnp.arange(CENT_DEV, dtype=jnp.int32)[None, None, :]).astype(jnp.float32)
    counts = jnp.sum(member, axis=1)
    centroid = jnp.einsum('ntc,ntd->ncd', member, tok_blocks.astype(jnp.float32)) / counts[:, :, None]
    grad_sum = jnp.einsum('ntc,ntd->ncd', member, grad_blocks.astype(jnp.float32))
    cent_in = centroid.astype(jnp.bfloat16)
    grad_in = grad_sum.astype(jnp.bfloat16)
    routed = routes.reshape(blocks, pair_count).astype(jnp.int32)
    matches = (routed[:, :, None] == jnp.arange(EXPERTS, dtype=jnp.int32)[None, None, :]).astype(jnp.int32)
    earlier = jnp.cumsum(matches, axis=1) - matches
    position = jnp.sum(earlier * matches, axis=2).astype(jnp.int32)
    slot_of = routed * CAP + position
    block_index = jnp.broadcast_to(jnp.arange(blocks, dtype=jnp.int32)[:, None], (blocks, pair_count))
    centroid_index = jnp.broadcast_to((jnp.arange(pair_count, dtype=jnp.int32) // TOP)[None, :], (blocks, pair_count))
    holders = jnp.full((blocks, EXPERTS * CAP), CENT_DEV, jnp.int32).at[block_index, slot_of].set(centroid_index)
    holders = jnp.transpose(holders.reshape(blocks, EXPERTS, CAP), (1, 0, 2))
    padded_cent = jnp.concatenate([cent_in, jnp.zeros((blocks, 1, D), jnp.bfloat16)], axis=1)
    padded_grad = jnp.concatenate([grad_in, jnp.zeros((blocks, 1, D), jnp.bfloat16)], axis=1)
    block_column = jnp.arange(blocks, dtype=jnp.int32)[:, None]

    def expert_step(bundle):
        holder, gate_mat, up_mat, down_mat = bundle
        inputs = padded_cent[block_column, holder].reshape(-1, D)
        incoming = padded_grad[block_column, holder].reshape(-1, D)
        gate_act = jnp.dot(inputs, gate_mat, preferred_element_type=jnp.float32)
        up_act = jnp.dot(inputs, up_mat, preferred_element_type=jnp.float32)
        sigmoid_gate = jax.nn.sigmoid(gate_act)
        hidden = (gate_act * sigmoid_gate * up_act).astype(jnp.bfloat16)
        output = jnp.dot(hidden, down_mat, preferred_element_type=jnp.float32).astype(jnp.bfloat16)
        hidden_grad = jnp.dot(incoming, down_mat.T, preferred_element_type=jnp.float32)
        gate_grad = (hidden_grad * up_act * sigmoid_gate * (1.0 + gate_act * (1.0 - sigmoid_gate))).astype(jnp.bfloat16)
        up_grad = (hidden_grad * gate_act * sigmoid_gate).astype(jnp.bfloat16)
        summed = jnp.dot(gate_grad, gate_mat.T, preferred_element_type=jnp.float32) + jnp.dot(up_grad, up_mat.T, preferred_element_type=jnp.float32)
        return output.reshape(blocks, CAP, D), summed.astype(jnp.bfloat16).reshape(blocks, CAP, D)

    outputs_all, grads_all = lax.map(expert_step, (holders, gate_weight, up_weight, down_weight))
    returned = outputs_all[routed, block_index, position].reshape(blocks, CENT_DEV, TOP, D)
    returned_grad = grads_all[routed, block_index, position].reshape(blocks, CENT_DEV, TOP, D)
    weights = route_weights.reshape(blocks, CENT_DEV, TOP)
    combined = jnp.sum(weights[:, :, :, None] * returned.astype(jnp.float32), axis=2)
    centroid_grad = jnp.sum(weights[:, :, :, None] * returned_grad.astype(jnp.float32), axis=2) - grad_sum
    layer_out = tok_blocks.astype(jnp.float32) + (combined - centroid)[block_column, cluster_blocks]
    token_grad = grad_blocks.astype(jnp.float32) + (centroid_grad / counts[:, :, None])[block_column, cluster_blocks]
    return layer_out.reshape(TOKENS, D), token_grad.reshape(TOKENS, D)
```

```python
import jax
import jax.numpy as jnp
from jax import lax
from jax.sharding import PartitionSpec as P


def expert_forward(inputs, gate_mat, up_mat, down_mat):
    gate_act = jnp.dot(inputs, gate_mat, preferred_element_type=jnp.float32)
    up_act = jnp.dot(inputs, up_mat, preferred_element_type=jnp.float32)
    sigmoid_gate = jax.nn.sigmoid(gate_act)
    hidden = (gate_act * sigmoid_gate * up_act).astype(jnp.bfloat16)
    output = jnp.dot(hidden, down_mat, preferred_element_type=jnp.float32).astype(jnp.bfloat16)
    return (output, gate_act, up_act)


def expert_backward(incoming, gate_act, up_act, gate_mat, up_mat, down_mat):
    against = (((1,), (1,)), ((), ()))
    hidden_grad = lax.dot_general(incoming, down_mat, against, preferred_element_type=jnp.float32)
    sigmoid_gate = jax.nn.sigmoid(gate_act)
    gate_grad = (
        hidden_grad * up_act * sigmoid_gate * (1.0 + gate_act * (1.0 - sigmoid_gate))
    ).astype(jnp.bfloat16)
    up_grad = (hidden_grad * gate_act * sigmoid_gate).astype(jnp.bfloat16)
    summed = lax.dot_general(gate_grad, gate_mat, against, preferred_element_type=jnp.float32)
    summed = summed + lax.dot_general(up_grad, up_mat, against, preferred_element_type=jnp.float32)
    return summed.astype(jnp.bfloat16)


def per_device(
    tokens, out_grad, cluster_ids, routes, route_weights, gate_weight, up_weight, down_weight
):
    model_width = tokens.shape[1]
    cent_rows = routes.shape[0]
    fanout = routes.shape[1]
    experts = lax.axis_size("expert")
    capacity = min(cent_rows, 2 * cent_rows * fanout // experts)
    member = (cluster_ids[:, None] == jnp.arange(cent_rows, dtype=jnp.int32)[None, :]).astype(
        jnp.bfloat16
    )
    counts = jnp.sum(member.astype(jnp.float32), axis=0)
    contract = (((0,), (0,)), ((), ()))
    centroid = (
        lax.dot_general(member, tokens, contract, preferred_element_type=jnp.float32)
        / counts[:, None]
    )
    grad_sum = lax.dot_general(member, out_grad, contract, preferred_element_type=jnp.float32)
    pair_ids = routes.reshape(-1)
    matches = (pair_ids[:, None] == jnp.arange(experts, dtype=jnp.int32)[None, :]).astype(jnp.int32)
    earlier = jnp.cumsum(matches, axis=0) - matches
    position = jnp.sum(earlier * matches, axis=1)
    slot_of = (pair_ids * capacity + position).reshape(cent_rows, fanout)
    slot_range = jnp.arange(experts * capacity, dtype=jnp.int32)
    placing = jnp.any(slot_of[None, :, :] == slot_range[:, None, None], axis=2).astype(jnp.bfloat16)
    send_cent = jnp.dot(placing, centroid.astype(jnp.bfloat16), preferred_element_type=jnp.float32)
    send_cent = send_cent.astype(jnp.bfloat16).reshape(experts, capacity, model_width)
    send_grad = jnp.dot(placing, grad_sum.astype(jnp.bfloat16), preferred_element_type=jnp.float32)
    send_grad = send_grad.astype(jnp.bfloat16).reshape(experts, capacity, model_width)
    gate_mat = gate_weight[0]
    up_mat = up_weight[0]
    down_mat = down_weight[0]
    arrived = lax.all_to_all(send_cent, "expert", split_axis=0, concat_axis=0, tiled=True)
    output, gate_act, up_act = expert_forward(
        arrived.reshape(-1, model_width), gate_mat, up_mat, down_mat
    )
    results = lax.all_to_all(
        output.reshape(experts, capacity, model_width),
        "expert",
        split_axis=0,
        concat_axis=0,
        tiled=True,
    )
    arrived_grad = lax.all_to_all(send_grad, "expert", split_axis=0, concat_axis=0, tiled=True)
    input_grad = expert_backward(
        arrived_grad.reshape(-1, model_width), gate_act, up_act, gate_mat, up_mat, down_mat
    )
    results_grad = lax.all_to_all(
        input_grad.reshape(experts, capacity, model_width),
        "expert",
        split_axis=0,
        concat_axis=0,
        tiled=True,
    )
    returned = results.reshape(-1, model_width)[slot_of]
    returned_grad = results_grad.reshape(-1, model_width)[slot_of]
    combined = jnp.sum(route_weights[:, :, None] * returned.astype(jnp.float32), axis=1)
    centroid_grad = (
        jnp.sum(route_weights[:, :, None] * returned_grad.astype(jnp.float32), axis=1) - grad_sum
    )
    layer_out = tokens.astype(jnp.float32) + jnp.take(combined - centroid, cluster_ids, axis=0)
    token_grad = out_grad.astype(jnp.float32) + jnp.take(
        centroid_grad / counts[:, None], cluster_ids, axis=0
    )
    return (layer_out, token_grad)


def dense_per_device(
    tokens, out_grad, cluster_ids, routes, route_weights, gate_weight, up_weight, down_weight
):
    cent_rows = routes.shape[0]
    experts = lax.axis_size("expert")
    me = lax.axis_index("expert")
    member = (cluster_ids[:, None] == jnp.arange(cent_rows, dtype=jnp.int32)[None, :]).astype(
        jnp.bfloat16
    )
    counts = jnp.sum(member.astype(jnp.float32), axis=0)
    contract = (((0,), (0,)), ((), ()))
    centroid = (
        lax.dot_general(member, tokens, contract, preferred_element_type=jnp.float32)
        / counts[:, None]
    )
    grad_sum = lax.dot_general(member, out_grad, contract, preferred_element_type=jnp.float32)
    spread = jnp.sum(
        jnp.where(
            routes[:, :, None] == jnp.arange(experts, dtype=jnp.int32)[None, None, :],
            route_weights[:, :, None],
            0.0,
        ),
        axis=1,
    )
    share = lax.all_gather(spread, "expert", axis=0, tiled=True)
    mine = lax.dynamic_slice_in_dim(share, me, 1, axis=1)
    arrived = lax.all_gather(centroid.astype(jnp.bfloat16), "expert", axis=0, tiled=True)
    arrived_grad = lax.all_gather(grad_sum.astype(jnp.bfloat16), "expert", axis=0, tiled=True)
    gate_mat = gate_weight[0]
    up_mat = up_weight[0]
    down_mat = down_weight[0]
    output, gate_act, up_act = expert_forward(arrived, gate_mat, up_mat, down_mat)
    combined = lax.psum_scatter(
        output.astype(jnp.float32) * mine, "expert", scatter_dimension=0, tiled=True
    )
    input_grad = expert_backward(arrived_grad, gate_act, up_act, gate_mat, up_mat, down_mat)
    centroid_grad = (
        lax.psum_scatter(
            input_grad.astype(jnp.float32) * mine, "expert", scatter_dimension=0, tiled=True
        )
        - grad_sum
    )
    layer_out = tokens.astype(jnp.float32) + jnp.take(combined - centroid, cluster_ids, axis=0)
    token_grad = out_grad.astype(jnp.float32) + jnp.take(
        centroid_grad / counts[:, None], cluster_ids, axis=0
    )
    return (layer_out, token_grad)


def solution(mesh):
    placed = (
        P(("groups", "expert"), None),
        P(("groups", "expert"), None),
        P(("groups", "expert")),
        P(("groups", "expert"), None),
        P(("groups", "expert"), None),
        P("expert", None, None),
        P("expert", None, None),
        P("expert", None, None),
    )
    dense = mesh.shape["expert"] <= 16
    return jax.shard_map(
        dense_per_device if dense else per_device,
        mesh=mesh,
        in_specs=placed,
        out_specs=(P(("groups", "expert"), None), P(("groups", "expert"), None)),
        check_vma=False,
    )
```

```python
import functools
import jax
import jax.numpy as jnp
from jax import lax
from jax.experimental import pallas as pl
from jax.experimental.pallas import tpu as pltpu
from jax.sharding import PartitionSpec as P


def expert_forward(inputs, gate_mat, up_mat, down_mat):
    gate_act = jnp.dot(inputs, gate_mat, preferred_element_type=jnp.float32)
    up_act = jnp.dot(inputs, up_mat, preferred_element_type=jnp.float32)
    sigmoid_gate = jax.nn.sigmoid(gate_act)
    hidden = (gate_act * sigmoid_gate * up_act).astype(jnp.bfloat16)
    output = jnp.dot(hidden, down_mat, preferred_element_type=jnp.float32).astype(jnp.bfloat16)
    return (output, gate_act, up_act)


def expert_backward(incoming, gate_act, up_act, gate_mat, up_mat, down_mat):
    against = (((1,), (1,)), ((), ()))
    hidden_grad = lax.dot_general(incoming, down_mat, against, preferred_element_type=jnp.float32)
    sigmoid_gate = jax.nn.sigmoid(gate_act)
    gate_grad = (
        hidden_grad * up_act * sigmoid_gate * (1.0 + gate_act * (1.0 - sigmoid_gate))
    ).astype(jnp.bfloat16)
    up_grad = (hidden_grad * gate_act * sigmoid_gate).astype(jnp.bfloat16)
    summed = lax.dot_general(gate_grad, gate_mat, against, preferred_element_type=jnp.float32)
    summed = summed + lax.dot_general(up_grad, up_mat, against, preferred_element_type=jnp.float32)
    return summed.astype(jnp.bfloat16)


def per_device(
    tokens, out_grad, cluster_ids, routes, route_weights, gate_weight, up_weight, down_weight
):
    model_width = tokens.shape[1]
    cent_rows = routes.shape[0]
    fanout = routes.shape[1]
    experts = lax.axis_size("expert")
    capacity = min(cent_rows, 2 * cent_rows * fanout // experts)
    member = (cluster_ids[:, None] == jnp.arange(cent_rows, dtype=jnp.int32)[None, :]).astype(
        jnp.bfloat16
    )
    counts = jnp.sum(member.astype(jnp.float32), axis=0)
    contract = (((0,), (0,)), ((), ()))
    centroid = (
        lax.dot_general(member, tokens, contract, preferred_element_type=jnp.float32)
        / counts[:, None]
    )
    grad_sum = lax.dot_general(member, out_grad, contract, preferred_element_type=jnp.float32)
    pair_ids = routes.reshape(-1)
    matches = (pair_ids[:, None] == jnp.arange(experts, dtype=jnp.int32)[None, :]).astype(jnp.int32)
    earlier = jnp.cumsum(matches, axis=0) - matches
    position = jnp.sum(earlier * matches, axis=1)
    slot_of = (pair_ids * capacity + position).reshape(cent_rows, fanout)
    slot_range = jnp.arange(experts * capacity, dtype=jnp.int32)
    placing = jnp.any(slot_of[None, :, :] == slot_range[:, None, None], axis=2).astype(jnp.bfloat16)
    send_cent = jnp.dot(placing, centroid.astype(jnp.bfloat16), preferred_element_type=jnp.float32)
    send_cent = send_cent.astype(jnp.bfloat16).reshape(experts, capacity, model_width)
    send_grad = jnp.dot(placing, grad_sum.astype(jnp.bfloat16), preferred_element_type=jnp.float32)
    send_grad = send_grad.astype(jnp.bfloat16).reshape(experts, capacity, model_width)
    gate_mat = gate_weight[0]
    up_mat = up_weight[0]
    down_mat = down_weight[0]
    arrived = lax.all_to_all(send_cent, "expert", split_axis=0, concat_axis=0, tiled=True)
    output, gate_act, up_act = expert_forward(
        arrived.reshape(-1, model_width), gate_mat, up_mat, down_mat
    )
    results = lax.all_to_all(
        output.reshape(experts, capacity, model_width),
        "expert",
        split_axis=0,
        concat_axis=0,
        tiled=True,
    )
    arrived_grad = lax.all_to_all(send_grad, "expert", split_axis=0, concat_axis=0, tiled=True)
    input_grad = expert_backward(
        arrived_grad.reshape(-1, model_width), gate_act, up_act, gate_mat, up_mat, down_mat
    )
    results_grad = lax.all_to_all(
        input_grad.reshape(experts, capacity, model_width),
        "expert",
        split_axis=0,
        concat_axis=0,
        tiled=True,
    )
    returned = results.reshape(-1, model_width)[slot_of]
    returned_grad = results_grad.reshape(-1, model_width)[slot_of]
    combined = jnp.sum(route_weights[:, :, None] * returned.astype(jnp.float32), axis=1)
    centroid_grad = (
        jnp.sum(route_weights[:, :, None] * returned_grad.astype(jnp.float32), axis=1) - grad_sum
    )
    layer_out = tokens.astype(jnp.float32) + jnp.take(combined - centroid, cluster_ids, axis=0)
    token_grad = out_grad.astype(jnp.float32) + jnp.take(
        centroid_grad / counts[:, None], cluster_ids, axis=0
    )
    return (layer_out, token_grad)


AGAINST = (((1,), (1,)), ((), ()))


def ring_layout(ring):
    half = ring // 2
    places = {}
    for hop in range(1, half):
        places[hop] = 2 * (hop - 1)
        places[-hop] = 2 * (hop - 1) + 1
    places[0] = ring - 2
    places[half] = ring - 1
    places[-half] = ring - 1
    return places


def exchange_kernel(
    experts,
    ids_ref,
    tokens_ref,
    out_grad_ref,
    routes_ref,
    route_weights_ref,
    gate_ref,
    up_ref,
    down_ref,
    delta_ref,
    delta_grad_ref,
    cent_all,
    grad_all,
    gate_up,
    down,
    hidden,
    hidden_grads,
    part_cent,
    part_grad,
    twin_cent,
    twin_grad,
    outgoing,
    incoming,
    centroid_keep,
    grad_keep,
    weight_sems,
    gather_send,
    gather_recv,
    share_send,
    share_recv,
    twin_send,
    twin_recv,
    ring_send,
    ring_recv,
):
    rows = routes_ref.shape[0]
    fanout = routes_ref.shape[1]
    width = tokens_ref.shape[1]
    hidden_width = down.shape[0]
    ring = experts // 2
    half = ring // 2
    places = ring_layout(ring)
    chunk = 4 * rows
    gathered = (cent_all, grad_all)
    parts = (part_cent, part_grad)
    twins = (twin_cent, twin_grad)

    me = lax.axis_index("expert")
    core = me % 2
    chip = me // 2
    column = chip % 2
    height = chip // 2
    spot = height + column * (ring - 1 - 2 * height)

    def device_at(position):
        side = position // half
        level = position + side * (ring - 1 - 2 * position)
        return (level * 2 + side) * 2 + core

    neighbour = (device_at((spot + 1) % ring), device_at((spot + ring - 1) % ring))
    twin = chip * 2 + (1 - core)

    weight_copies = [
        pltpu.make_async_copy(
            gate_ref.at[0], gate_up.at[:, pl.ds(0, hidden_width)], weight_sems.at[0]
        ),
        pltpu.make_async_copy(
            up_ref.at[0], gate_up.at[:, pl.ds(hidden_width, hidden_width)], weight_sems.at[1]
        ),
        pltpu.make_async_copy(down_ref.at[0], down, weight_sems.at[2]),
    ]
    for copy in weight_copies:
        copy.start()

    barrier = pltpu.get_barrier_semaphore()
    for other in (neighbour[0], neighbour[1], twin):
        pl.semaphore_signal(
            barrier, inc=1, device_id={"expert": other}, device_id_type=pl.DeviceIdType.MESH
        )

    def block(distance, which):
        return pl.ds((places[distance] * 2 + which) * rows, rows)

    members = (
        lax.broadcasted_iota(jnp.int32, (rows, ids_ref.shape[1]), 0) == ids_ref[...]
    ).astype(jnp.float32)
    counts = jnp.sum(members, axis=1, keepdims=True)
    members = members.astype(jnp.bfloat16)
    centroid = jnp.dot(members, tokens_ref[...], preferred_element_type=jnp.float32) / counts
    grad_sum = jnp.dot(members, out_grad_ref[...], preferred_element_type=jnp.float32)
    centroid_keep[...] = centroid
    grad_keep[...] = grad_sum
    cent_all[block(0, 0), pl.ds(0, width)] = centroid.astype(jnp.bfloat16)
    grad_all[block(0, 0), :] = grad_sum.astype(jnp.bfloat16)

    lanes = lax.broadcasted_iota(jnp.int32, (rows, 128), 1)
    spread = jnp.zeros((rows, 128), jnp.float32)
    for k in range(fanout):
        spread = spread + jnp.where(
            lanes % experts == routes_ref[:, k : k + 1], route_weights_ref[:, k : k + 1], 0.0
        )
    high = spread.astype(jnp.bfloat16).astype(jnp.float32)
    middle = (spread - high).astype(jnp.bfloat16).astype(jnp.float32)
    low = spread - high - middle
    pieces = jnp.where(lanes < experts, high, jnp.where(lanes < 2 * experts, middle, low))
    cent_all[block(0, 0), pl.ds(width, 128)] = pieces.astype(jnp.bfloat16)

    def remote(source, target, send, recv, other):
        return pltpu.make_async_remote_copy(
            src_ref=source,
            dst_ref=target,
            send_sem=send,
            recv_sem=recv,
            device_id={"expert": other},
            device_id_type=pl.DeviceIdType.MESH,
        )

    def signed(way, distance):
        return -distance if way == 0 else distance

    def hops_of(kind, way):
        return half if kind == way else half - 1

    def gather_copy(kind, way, hop):
        return remote(
            gathered[kind].at[block(signed(way, hop - 1), 0), :],
            gathered[kind].at[block(signed(way, hop), 0), :],
            gather_send.at[kind, way, hop - 1],
            gather_recv.at[kind, way, hop - 1],
            neighbour[way],
        )

    def share_copy(kind, distance):
        return remote(
            gathered[kind].at[block(distance, 0), :],
            gathered[kind].at[block(distance, 1), :],
            share_send.at[kind, places[distance]],
            share_recv.at[kind, places[distance]],
            twin,
        )

    def twin_copy(kind, distance):
        return remote(
            parts[kind].at[block(distance, 1), :],
            twins[kind].at[pl.ds(places[distance] * rows, rows), :],
            twin_send.at[kind, places[distance]],
            twin_recv.at[kind, places[distance]],
            twin,
        )

    def ring_copy(kind, way, step):
        return remote(
            outgoing.at[kind, way, step - 1],
            incoming.at[kind, way, step - 1],
            ring_send.at[kind, way, step - 1],
            ring_recv.at[kind, way, step - 1],
            neighbour[way],
        )

    started = []

    def start(copy):
        copy.start()
        started.append(copy)

    pl.semaphore_wait(barrier, 3)
    for way in range(2):
        for kind in range(2):
            start(gather_copy(kind, way, 1))
    for kind in range(2):
        start(share_copy(kind, 0))

    tile = 256 if hidden_width % 256 == 0 else hidden_width
    wide = 512 if width % 512 == 0 else width

    def compute(number):
        first = number * chunk
        span = pl.ds(first, chunk)
        pieces = cent_all[span, pl.ds(width, 128)].astype(jnp.float32)
        lanes = lax.broadcasted_iota(jnp.int32, (chunk, 128), 1)
        own = (lanes % experts == me) & (lanes < 3 * experts)
        weight = jnp.sum(jnp.where(own, pieces, 0.0), axis=1, keepdims=True)

        def inner(j, carry):
            columns = pl.ds(pl.multiple_of(j * tile, tile), tile)
            later = pl.ds(pl.multiple_of(hidden_width + j * tile, tile), tile)
            inputs = cent_all[span, pl.ds(0, width)]
            gate_act = jnp.dot(inputs, gate_up[:, columns], preferred_element_type=jnp.float32)
            up_act = jnp.dot(inputs, gate_up[:, later], preferred_element_type=jnp.float32)
            grads = lax.dot_general(
                grad_all[span, :], down[columns, :], AGAINST, preferred_element_type=jnp.float32
            )
            sigmoid_gate = jax.nn.sigmoid(gate_act)
            hidden[:, columns] = (gate_act * sigmoid_gate * up_act).astype(jnp.bfloat16)
            hidden_grads[:, columns] = (
                grads * up_act * sigmoid_gate * (1.0 + gate_act * (1.0 - sigmoid_gate))
            ).astype(jnp.bfloat16)
            hidden_grads[:, later] = (grads * gate_act * sigmoid_gate).astype(jnp.bfloat16)
            return carry

        lax.fori_loop(0, hidden_width // tile, inner, 0)

        def outer(t, carry):
            columns = pl.ds(pl.multiple_of(t * wide, wide), wide)
            output = jnp.dot(hidden[...], down[:, columns], preferred_element_type=jnp.float32)
            output = output.astype(jnp.bfloat16).astype(jnp.float32)
            part_cent[span, columns] = output * weight
            summed = lax.dot_general(
                hidden_grads[...],
                gate_up[columns, :],
                AGAINST,
                preferred_element_type=jnp.float32,
            )
            summed = summed.astype(jnp.bfloat16).astype(jnp.float32)
            part_grad[span, columns] = summed * weight
            return carry

        lax.fori_loop(0, width // wide, outer, 0)

    def contribution(kind, distance):
        twin_copy(kind, distance).wait_recv()
        return (
            parts[kind][block(distance, 0), :]
            + twins[kind][pl.ds(places[distance] * rows, rows), :]
        )

    def toward(way, distance):
        return distance if way == 0 else -distance

    def send_first(kind, way):
        total = contribution(kind, toward(way, hops_of(kind, way)))
        outgoing[kind, way, 0] = total.astype(jnp.bfloat16)
        start(ring_copy(kind, way, 1))

    for hop in range(1, half + 1):
        for kind in range(2):
            for way in range(2):
                if hop <= hops_of(kind, way):
                    gather_copy(kind, way, hop).wait_recv()
                    if hop < hops_of(kind, way):
                        start(gather_copy(kind, way, hop + 1))
                    start(share_copy(kind, signed(way, hop)))
        if hop == 1:
            for copy in weight_copies:
                copy.wait()
        if hop == half:
            for kind in range(2):
                send_first(kind, 1 - kind)
        distances = (hop, -hop) if hop < half else (half, 0)
        for kind in range(2):
            for distance in distances:
                share_copy(kind, distance).wait_recv()
        compute(hop - 1)
        for distance in distances:
            for kind in range(2):
                start(twin_copy(kind, distance))

    for kind in range(2):
        send_first(kind, kind)
    totals = [contribution(kind, 0) for kind in range(2)]
    delta_ref[...] = totals[0] - centroid_keep[...]
    delta_grad_ref[...] = totals[1] - grad_keep[...]
    for step in range(1, half + 1):
        for kind in range(2):
            for way in (1 - kind, kind):
                hops = hops_of(kind, way)
                if step > hops:
                    continue
                ring_copy(kind, way, step).wait_recv()
                arrived = incoming[kind, way, step - 1].astype(jnp.float32)
                if step < hops:
                    total = arrived + contribution(kind, toward(way, hops - step))
                    outgoing[kind, way, step] = total.astype(jnp.bfloat16)
                    start(ring_copy(kind, way, step + 1))
                elif kind == 0:
                    delta_ref[...] += arrived
                else:
                    delta_grad_ref[...] += arrived
    delta_grad_ref[...] = delta_grad_ref[...] / counts
    for copy in started:
        copy.wait_send()


def decode_kernel(ids_ref, tokens_ref, out_grad_ref, delta_ref, delta_grad_ref, out_ref, grad_ref):
    rows = delta_ref.shape[0]
    members = (
        lax.broadcasted_iota(jnp.int32, (rows, ids_ref.shape[1]), 0) == ids_ref[...]
    ).astype(jnp.bfloat16)
    contract = (((0,), (0,)), ((), ()))

    def spread(table):
        high = table.astype(jnp.bfloat16)
        rest = table - high.astype(jnp.float32)
        middle = rest.astype(jnp.bfloat16)
        low = (rest - middle.astype(jnp.float32)).astype(jnp.bfloat16)
        total = lax.dot_general(members, high, contract, preferred_element_type=jnp.float32)
        total += lax.dot_general(members, middle, contract, preferred_element_type=jnp.float32)
        return total + lax.dot_general(members, low, contract, preferred_element_type=jnp.float32)

    out_ref[...] = tokens_ref[...].astype(jnp.float32) + spread(delta_ref[...])
    grad_ref[...] = out_grad_ref[...].astype(jnp.float32) + spread(delta_grad_ref[...])


def ring_per_device(
    tokens, out_grad, cluster_ids, routes, route_weights, gate_weight, up_weight, down_weight
):
    experts = lax.axis_size("expert")
    rows = routes.shape[0]
    count, width = tokens.shape
    hidden_width = gate_weight.shape[2]
    ring = experts // 2
    half = ring // 2
    held = experts * rows
    ids = cluster_ids.reshape(1, count)
    vmem = pl.BlockSpec(memory_space=pltpu.VMEM)
    anywhere = pl.BlockSpec(memory_space=pl.ANY)
    table = jax.ShapeDtypeStruct((rows, width), jnp.float32)
    bf16, f32, dma = jnp.bfloat16, jnp.float32, pltpu.SemaphoreType.DMA
    delta, delta_grad = pl.pallas_call(
        functools.partial(exchange_kernel, experts),
        out_shape=(table, table),
        in_specs=[vmem] * 5 + [anywhere] * 3,
        out_specs=(vmem, vmem),
        scratch_shapes=[
            pltpu.VMEM((held, width + 128), bf16),
            pltpu.VMEM((held, width), bf16),
            pltpu.VMEM((width, 2 * hidden_width), bf16),
            pltpu.VMEM((hidden_width, width), bf16),
            pltpu.VMEM((4 * rows, hidden_width), bf16),
            pltpu.VMEM((4 * rows, 2 * hidden_width), bf16),
            pltpu.VMEM((held, width), f32),
            pltpu.VMEM((held, width), f32),
            pltpu.VMEM((ring * rows, width), f32),
            pltpu.VMEM((ring * rows, width), f32),
            pltpu.VMEM((2, 2, half, rows, width), bf16),
            pltpu.VMEM((2, 2, half, rows, width), bf16),
            pltpu.VMEM((rows, width), f32),
            pltpu.VMEM((rows, width), f32),
            dma((3,)),
            dma((2, 2, half)),
            dma((2, 2, half)),
            dma((2, ring)),
            dma((2, ring)),
            dma((2, ring)),
            dma((2, ring)),
            dma((2, 2, half)),
            dma((2, 2, half)),
        ],
        compiler_params=pltpu.CompilerParams(
            collective_id=0, has_side_effects=True, vmem_limit_bytes=56 * 1024 * 1024
        ),
        cost_estimate=pl.CostEstimate(
            flops=12 * held * width * hidden_width,
            bytes_accessed=6 * width * hidden_width,
            transcendentals=held * hidden_width,
        ),
    )(ids, tokens, out_grad, routes, route_weights, gate_weight, up_weight, down_weight)
    step = 512 if width % 512 == 0 else width
    whole = pl.BlockSpec((1, count), lambda i: (0, 0))
    tall = pl.BlockSpec((count, step), lambda i: (0, i))
    short = pl.BlockSpec((rows, step), lambda i: (0, i))
    result = jax.ShapeDtypeStruct((count, width), jnp.float32)
    return pl.pallas_call(
        decode_kernel,
        grid=(width // step,),
        out_shape=(result, result),
        in_specs=[whole, tall, tall, short, short],
        out_specs=(tall, tall),
    )(ids, tokens, out_grad, delta, delta_grad)


def solution(mesh):
    placed = (
        P(("groups", "expert"), None),
        P(("groups", "expert"), None),
        P(("groups", "expert")),
        P(("groups", "expert"), None),
        P(("groups", "expert"), None),
        P("expert", None, None),
        P("expert", None, None),
        P("expert", None, None),
    )
    size = mesh.shape["expert"]
    ringed = size % 4 == 0 and 8 <= size <= 32
    return jax.shard_map(
        ring_per_device if ringed else per_device,
        mesh=mesh,
        in_specs=placed,
        out_specs=(P(("groups", "expert"), None), P(("groups", "expert"), None)),
        check_vma=False,
    )
```

```python
import functools
import jax
import jax.numpy as jnp
from jax import lax
from jax.experimental import pallas as pl
from jax.experimental.pallas import tpu as pltpu
from jax.sharding import PartitionSpec as P


def expert_forward(inputs, gate_mat, up_mat, down_mat):
    gate_act = jnp.dot(inputs, gate_mat, preferred_element_type=jnp.float32)
    up_act = jnp.dot(inputs, up_mat, preferred_element_type=jnp.float32)
    sigmoid_gate = jax.nn.sigmoid(gate_act)
    hidden = (gate_act * sigmoid_gate * up_act).astype(jnp.bfloat16)
    output = jnp.dot(hidden, down_mat, preferred_element_type=jnp.float32).astype(jnp.bfloat16)
    return (output, gate_act, up_act)


def expert_backward(incoming, gate_act, up_act, gate_mat, up_mat, down_mat):
    against = (((1,), (1,)), ((), ()))
    hidden_grad = lax.dot_general(incoming, down_mat, against, preferred_element_type=jnp.float32)
    sigmoid_gate = jax.nn.sigmoid(gate_act)
    gate_grad = (
        hidden_grad * up_act * sigmoid_gate * (1.0 + gate_act * (1.0 - sigmoid_gate))
    ).astype(jnp.bfloat16)
    up_grad = (hidden_grad * gate_act * sigmoid_gate).astype(jnp.bfloat16)
    summed = lax.dot_general(gate_grad, gate_mat, against, preferred_element_type=jnp.float32)
    summed = summed + lax.dot_general(up_grad, up_mat, against, preferred_element_type=jnp.float32)
    return summed.astype(jnp.bfloat16)


def per_device(
    tokens, out_grad, cluster_ids, routes, route_weights, gate_weight, up_weight, down_weight
):
    model_width = tokens.shape[1]
    cent_rows = routes.shape[0]
    fanout = routes.shape[1]
    experts = lax.axis_size("expert")
    capacity = min(cent_rows, 2 * cent_rows * fanout // experts)
    member = (cluster_ids[:, None] == jnp.arange(cent_rows, dtype=jnp.int32)[None, :]).astype(
        jnp.bfloat16
    )
    counts = jnp.sum(member.astype(jnp.float32), axis=0)
    contract = (((0,), (0,)), ((), ()))
    centroid = (
        lax.dot_general(member, tokens, contract, preferred_element_type=jnp.float32)
        / counts[:, None]
    )
    grad_sum = lax.dot_general(member, out_grad, contract, preferred_element_type=jnp.float32)
    pair_ids = routes.reshape(-1)
    matches = (pair_ids[:, None] == jnp.arange(experts, dtype=jnp.int32)[None, :]).astype(jnp.int32)
    earlier = jnp.cumsum(matches, axis=0) - matches
    position = jnp.sum(earlier * matches, axis=1)
    slot_of = (pair_ids * capacity + position).reshape(cent_rows, fanout)
    slot_range = jnp.arange(experts * capacity, dtype=jnp.int32)
    placing = jnp.any(slot_of[None, :, :] == slot_range[:, None, None], axis=2).astype(jnp.bfloat16)
    send_cent = jnp.dot(placing, centroid.astype(jnp.bfloat16), preferred_element_type=jnp.float32)
    send_cent = send_cent.astype(jnp.bfloat16).reshape(experts, capacity, model_width)
    send_grad = jnp.dot(placing, grad_sum.astype(jnp.bfloat16), preferred_element_type=jnp.float32)
    send_grad = send_grad.astype(jnp.bfloat16).reshape(experts, capacity, model_width)
    gate_mat = gate_weight[0]
    up_mat = up_weight[0]
    down_mat = down_weight[0]
    arrived = lax.all_to_all(send_cent, "expert", split_axis=0, concat_axis=0, tiled=True)
    output, gate_act, up_act = expert_forward(
        arrived.reshape(-1, model_width), gate_mat, up_mat, down_mat
    )
    results = lax.all_to_all(
        output.reshape(experts, capacity, model_width),
        "expert",
        split_axis=0,
        concat_axis=0,
        tiled=True,
    )
    arrived_grad = lax.all_to_all(send_grad, "expert", split_axis=0, concat_axis=0, tiled=True)
    input_grad = expert_backward(
        arrived_grad.reshape(-1, model_width), gate_act, up_act, gate_mat, up_mat, down_mat
    )
    results_grad = lax.all_to_all(
        input_grad.reshape(experts, capacity, model_width),
        "expert",
        split_axis=0,
        concat_axis=0,
        tiled=True,
    )
    returned = results.reshape(-1, model_width)[slot_of]
    returned_grad = results_grad.reshape(-1, model_width)[slot_of]
    combined = jnp.sum(route_weights[:, :, None] * returned.astype(jnp.float32), axis=1)
    centroid_grad = (
        jnp.sum(route_weights[:, :, None] * returned_grad.astype(jnp.float32), axis=1) - grad_sum
    )
    layer_out = tokens.astype(jnp.float32) + jnp.take(combined - centroid, cluster_ids, axis=0)
    token_grad = out_grad.astype(jnp.float32) + jnp.take(
        centroid_grad / counts[:, None], cluster_ids, axis=0
    )
    return (layer_out, token_grad)


AGAINST = (((1,), (1,)), ((), ()))


def ring_layout(ring):
    half = ring // 2
    places = {}
    for hop in range(1, half):
        places[hop] = 2 * (hop - 1)
        places[-hop] = 2 * (hop - 1) + 1
    places[0] = ring - 2
    places[half] = ring - 1
    places[-half] = ring - 1
    return places


def exchange_kernel(
    experts,
    ids_ref,
    tokens_ref,
    out_grad_ref,
    routes_ref,
    route_weights_ref,
    gate_ref,
    up_ref,
    down_ref,
    delta_ref,
    delta_grad_ref,
    cent_all,
    grad_all,
    gate_up,
    down,
    gate_up_turned,
    down_turned,
    hidden,
    hidden_grads,
    part_cent,
    part_grad,
    twin_cent,
    twin_grad,
    outgoing,
    incoming,
    centroid_keep,
    grad_keep,
    weight_sems,
    gather_send,
    gather_recv,
    share_send,
    share_recv,
    twin_send,
    twin_recv,
    ring_send,
    ring_recv,
):
    fanout, rows = routes_ref.shape
    width = tokens_ref.shape[1]
    hidden_width = down.shape[0]
    ring = experts // 2
    half = ring // 2
    places = ring_layout(ring)
    chunk = 4 * rows
    gathered = (cent_all, grad_all)
    parts = (part_cent, part_grad)
    twins = (twin_cent, twin_grad)

    me = lax.axis_index("expert")
    core = me % 2
    chip = me // 2
    column = chip % 2
    height = chip // 2
    spot = height + column * (ring - 1 - 2 * height)

    def device_at(position):
        side = position // half
        level = position + side * (ring - 1 - 2 * position)
        return (level * 2 + side) * 2 + core

    neighbour = (device_at((spot + 1) % ring), device_at((spot + ring - 1) % ring))
    twin = chip * 2 + (1 - core)

    weight_copies = [
        pltpu.make_async_copy(
            gate_ref.at[0], gate_up.at[:, pl.ds(0, hidden_width)], weight_sems.at[0]
        ),
        pltpu.make_async_copy(
            up_ref.at[0], gate_up.at[:, pl.ds(hidden_width, hidden_width)], weight_sems.at[1]
        ),
        pltpu.make_async_copy(down_ref.at[0], down, weight_sems.at[2]),
    ]
    for copy in weight_copies:
        copy.start()

    barrier = pltpu.get_barrier_semaphore()
    for other in (neighbour[0], neighbour[1], twin):
        pl.semaphore_signal(
            barrier, inc=1, device_id={"expert": other}, device_id_type=pl.DeviceIdType.MESH
        )

    def block(distance, which):
        return pl.ds((places[distance] * 2 + which) * rows, rows)

    members = (
        lax.broadcasted_iota(jnp.int32, (rows, ids_ref.shape[1]), 0) == ids_ref[...]
    ).astype(jnp.float32)
    counts = jnp.sum(members, axis=1, keepdims=True)
    members = members.astype(jnp.bfloat16)
    centroid = jnp.dot(members, tokens_ref[...], preferred_element_type=jnp.float32) / counts
    grad_sum = jnp.dot(members, out_grad_ref[...], preferred_element_type=jnp.float32)
    centroid_keep[...] = centroid
    grad_keep[...] = grad_sum
    cent_all[block(0, 0), pl.ds(0, width)] = centroid.astype(jnp.bfloat16)
    grad_all[block(0, 0), :] = grad_sum.astype(jnp.bfloat16)

    lanes = lax.broadcasted_iota(jnp.int32, (128, rows), 0)
    spread = jnp.zeros((128, rows), jnp.float32)
    for k in range(fanout):
        spread = spread + jnp.where(
            lanes % experts == routes_ref[k : k + 1, :], route_weights_ref[k : k + 1, :], 0.0
        )
    high = spread.astype(jnp.bfloat16).astype(jnp.float32)
    middle = (spread - high).astype(jnp.bfloat16).astype(jnp.float32)
    low = spread - high - middle
    pieces = jnp.where(lanes < experts, high, jnp.where(lanes < 2 * experts, middle, low))
    same = lax.broadcasted_iota(jnp.int32, (rows, rows), 0) == lax.broadcasted_iota(
        jnp.int32, (rows, rows), 1
    )
    pieces = lax.dot_general(
        same.astype(jnp.bfloat16),
        pieces.astype(jnp.bfloat16),
        AGAINST,
        preferred_element_type=jnp.float32,
    )
    cent_all[block(0, 0), pl.ds(width, 128)] = pieces.astype(jnp.bfloat16)

    def remote(source, target, send, recv, other):
        return pltpu.make_async_remote_copy(
            src_ref=source,
            dst_ref=target,
            send_sem=send,
            recv_sem=recv,
            device_id={"expert": other},
            device_id_type=pl.DeviceIdType.MESH,
        )

    def signed(way, distance):
        return -distance if way == 0 else distance

    def hops_of(kind, way):
        return half if kind == way else half - 1

    def gather_copy(kind, way, hop):
        return remote(
            gathered[kind].at[block(signed(way, hop - 1), 0), :],
            gathered[kind].at[block(signed(way, hop), 0), :],
            gather_send.at[kind, way, hop - 1],
            gather_recv.at[kind, way, hop - 1],
            neighbour[way],
        )

    def share_copy(kind, distance):
        return remote(
            gathered[kind].at[block(distance, 0), :],
            gathered[kind].at[block(distance, 1), :],
            share_send.at[kind, places[distance]],
            share_recv.at[kind, places[distance]],
            twin,
        )

    def twin_copy(kind, distance):
        return remote(
            parts[kind].at[block(distance, 1), :],
            twins[kind].at[pl.ds(places[distance] * rows, rows), :],
            twin_send.at[kind, places[distance]],
            twin_recv.at[kind, places[distance]],
            twin,
        )

    def ring_copy(kind, way, step):
        return remote(
            outgoing.at[kind, way, step - 1],
            incoming.at[kind, way, step - 1],
            ring_send.at[kind, way, step - 1],
            ring_recv.at[kind, way, step - 1],
            neighbour[way],
        )

    started = []

    def start(copy):
        copy.start()
        started.append(copy)

    pl.semaphore_wait(barrier, 3)
    for way in range(2):
        for kind in range(2):
            start(gather_copy(kind, way, 1))
    for kind in range(2):
        start(share_copy(kind, 0))

    tile = 256 if hidden_width % 256 == 0 else hidden_width
    wide = 512 if width % 512 == 0 else width

    def turn(source, target, first, last):
        across = source.shape[1] // tile

        def body(r, carry):
            lines = pl.ds(pl.multiple_of(r * tile, tile), tile)
            for c in range(across):
                columns = pl.ds(c * tile, tile)
                target[columns, lines] = source[lines, columns].T
            return carry

        lax.fori_loop(first, last, body, 0)

    def first_half(number):
        span = pl.ds(number * chunk, chunk)

        def inner(j, carry):
            columns = pl.ds(pl.multiple_of(j * tile, tile), tile)
            later = pl.ds(pl.multiple_of(hidden_width + j * tile, tile), tile)
            inputs = cent_all[span, pl.ds(0, width)]
            gate_act = jnp.dot(inputs, gate_up[:, columns], preferred_element_type=jnp.float32)
            up_act = jnp.dot(inputs, gate_up[:, later], preferred_element_type=jnp.float32)
            grads = jnp.dot(
                grad_all[span, :], down_turned[:, columns], preferred_element_type=jnp.float32
            )
            sigmoid_gate = jax.nn.sigmoid(gate_act)
            hidden[:, columns] = (gate_act * sigmoid_gate * up_act).astype(jnp.bfloat16)
            hidden_grads[:, columns] = (
                grads * up_act * sigmoid_gate * (1.0 + gate_act * (1.0 - sigmoid_gate))
            ).astype(jnp.bfloat16)
            hidden_grads[:, later] = (grads * gate_act * sigmoid_gate).astype(jnp.bfloat16)
            return carry

        lax.fori_loop(0, hidden_width // tile, inner, 0)

    def second_half(number):
        span = pl.ds(number * chunk, chunk)
        pieces = cent_all[span, pl.ds(width, 128)].astype(jnp.float32)
        lanes = lax.broadcasted_iota(jnp.int32, (chunk, 128), 1)
        own = (lanes % experts == me) & (lanes < 3 * experts)
        weight = jnp.sum(jnp.where(own, pieces, 0.0), axis=1, keepdims=True)

        def outer(t, carry):
            columns = pl.ds(pl.multiple_of(t * wide, wide), wide)
            output = jnp.dot(hidden[...], down[:, columns], preferred_element_type=jnp.float32)
            output = output.astype(jnp.bfloat16).astype(jnp.float32)
            part_cent[span, columns] = output * weight
            summed = jnp.dot(
                hidden_grads[...], gate_up_turned[:, columns], preferred_element_type=jnp.float32
            )
            summed = summed.astype(jnp.bfloat16).astype(jnp.float32)
            part_grad[span, columns] = summed * weight
            return carry

        lax.fori_loop(0, width // wide, outer, 0)

    def contribution(kind, distance):
        twin_copy(kind, distance).wait_recv()
        return (
            parts[kind][block(distance, 0), :]
            + twins[kind][pl.ds(places[distance] * rows, rows), :]
        )

    def toward(way, distance):
        return distance if way == 0 else -distance

    def send_first(kind, way):
        total = contribution(kind, toward(way, hops_of(kind, way)))
        outgoing[kind, way, 0] = total.astype(jnp.bfloat16)
        start(ring_copy(kind, way, 1))

    def pass_on(hop, kind):
        for way in range(2):
            if hop <= hops_of(kind, way):
                gather_copy(kind, way, hop).wait_recv()
                if hop < hops_of(kind, way):
                    start(gather_copy(kind, way, hop + 1))
                start(share_copy(kind, signed(way, hop)))

    def distances_of(hop):
        return (hop, -hop) if hop < half else (half, 0)

    def wait_shares(hop):
        for kind in range(2):
            for distance in distances_of(hop):
                share_copy(kind, distance).wait_recv()

    def start_twins(hop):
        for distance in distances_of(hop):
            for kind in range(2):
                start(twin_copy(kind, distance))

    bands = width // tile
    weight_copies[2].wait()
    turn(down, down_turned, 0, hidden_width // tile)
    pass_on(1, 0)
    weight_copies[0].wait()
    weight_copies[1].wait()
    turn(gate_up, gate_up_turned, 0, bands // 2)
    pass_on(1, 1)
    turn(gate_up, gate_up_turned, bands // 2, bands)
    for hop in range(1, half + 1):
        if hop < half:
            pass_on(hop + 1, 0)
        wait_shares(hop)
        first_half(hop - 1)
        if hop < half:
            pass_on(hop + 1, 1)
        else:
            for kind in range(2):
                send_first(kind, 1 - kind)
        second_half(hop - 1)
        start_twins(hop)

    for kind in range(2):
        send_first(kind, kind)
    totals = [contribution(kind, 0) for kind in range(2)]
    delta_ref[...] = totals[0] - centroid_keep[...]
    delta_grad_ref[...] = totals[1] - grad_keep[...]
    for step in range(1, half + 1):
        for kind in range(2):
            for way in (1 - kind, kind):
                hops = hops_of(kind, way)
                if step > hops:
                    continue
                ring_copy(kind, way, step).wait_recv()
                arrived = incoming[kind, way, step - 1].astype(jnp.float32)
                if step < hops:
                    total = arrived + contribution(kind, toward(way, hops - step))
                    outgoing[kind, way, step] = total.astype(jnp.bfloat16)
                    start(ring_copy(kind, way, step + 1))
                elif kind == 0:
                    delta_ref[...] += arrived
                else:
                    delta_grad_ref[...] += arrived
    delta_grad_ref[...] = delta_grad_ref[...] / counts
    for copy in started:
        copy.wait_send()


def decode_kernel(ids_ref, tokens_ref, out_grad_ref, delta_ref, delta_grad_ref, out_ref, grad_ref):
    rows = delta_ref.shape[0]
    lines = lax.broadcasted_iota(jnp.int32, (3 * rows, ids_ref.shape[1]), 0)
    members = (lines % rows == ids_ref[...]).astype(jnp.bfloat16)
    contract = (((0,), (0,)), ((), ()))

    def spread(table):
        high = table.astype(jnp.bfloat16)
        rest = table - high.astype(jnp.float32)
        middle = rest.astype(jnp.bfloat16)
        low = (rest - middle.astype(jnp.float32)).astype(jnp.bfloat16)
        stacked = jnp.concatenate([high, middle, low], axis=0)
        return lax.dot_general(members, stacked, contract, preferred_element_type=jnp.float32)

    out_ref[...] = tokens_ref[...].astype(jnp.float32) + spread(delta_ref[...])
    grad_ref[...] = out_grad_ref[...].astype(jnp.float32) + spread(delta_grad_ref[...])


def ring_per_device(
    tokens, out_grad, cluster_ids, routes, route_weights, gate_weight, up_weight, down_weight
):
    experts = lax.axis_size("expert")
    rows = routes.shape[0]
    count, width = tokens.shape
    hidden_width = gate_weight.shape[2]
    ring = experts // 2
    half = ring // 2
    held = experts * rows
    ids = cluster_ids.reshape(1, count)
    vmem = pl.BlockSpec(memory_space=pltpu.VMEM)
    anywhere = pl.BlockSpec(memory_space=pl.ANY)
    table = jax.ShapeDtypeStruct((rows, width), jnp.float32)
    bf16, f32, dma = jnp.bfloat16, jnp.float32, pltpu.SemaphoreType.DMA
    delta, delta_grad = pl.pallas_call(
        functools.partial(exchange_kernel, experts),
        out_shape=(table, table),
        in_specs=[vmem] * 5 + [anywhere] * 3,
        out_specs=(vmem, vmem),
        scratch_shapes=[
            pltpu.VMEM((held, width + 128), bf16),
            pltpu.VMEM((held, width), bf16),
            pltpu.VMEM((width, 2 * hidden_width), bf16),
            pltpu.VMEM((hidden_width, width), bf16),
            pltpu.VMEM((2 * hidden_width, width), bf16),
            pltpu.VMEM((width, hidden_width), bf16),
            pltpu.VMEM((4 * rows, hidden_width), bf16),
            pltpu.VMEM((4 * rows, 2 * hidden_width), bf16),
            pltpu.VMEM((held, width), f32),
            pltpu.VMEM((held, width), f32),
            pltpu.VMEM((ring * rows, width), f32),
            pltpu.VMEM((ring * rows, width), f32),
            pltpu.VMEM((2, 2, half, rows, width), bf16),
            pltpu.VMEM((2, 2, half, rows, width), bf16),
            pltpu.VMEM((rows, width), f32),
            pltpu.VMEM((rows, width), f32),
            dma((3,)),
            dma((2, 2, half)),
            dma((2, 2, half)),
            dma((2, ring)),
            dma((2, ring)),
            dma((2, ring)),
            dma((2, ring)),
            dma((2, 2, half)),
            dma((2, 2, half)),
        ],
        compiler_params=pltpu.CompilerParams(
            collective_id=0, has_side_effects=True, vmem_limit_bytes=56 * 1024 * 1024
        ),
        cost_estimate=pl.CostEstimate(
            flops=12 * held * width * hidden_width,
            bytes_accessed=6 * width * hidden_width,
            transcendentals=held * hidden_width,
        ),
    )(ids, tokens, out_grad, routes.T, route_weights.T, gate_weight, up_weight, down_weight)
    step = 512 if width % 512 == 0 else width
    whole = pl.BlockSpec((1, count), lambda i: (0, 0))
    tall = pl.BlockSpec((count, step), lambda i: (0, i))
    short = pl.BlockSpec((rows, step), lambda i: (0, i))
    result = jax.ShapeDtypeStruct((count, width), jnp.float32)
    return pl.pallas_call(
        decode_kernel,
        grid=(width // step,),
        out_shape=(result, result),
        in_specs=[whole, tall, tall, short, short],
        out_specs=(tall, tall),
    )(ids, tokens, out_grad, delta, delta_grad)


def solution(mesh):
    placed = (
        P(("groups", "expert"), None),
        P(("groups", "expert"), None),
        P(("groups", "expert")),
        P(("groups", "expert"), None),
        P(("groups", "expert"), None),
        P("expert", None, None),
        P("expert", None, None),
        P("expert", None, None),
    )
    size = mesh.shape["expert"]
    ringed = size % 4 == 0 and 8 <= size <= 32
    return jax.shard_map(
        ring_per_device if ringed else per_device,
        mesh=mesh,
        in_specs=placed,
        out_specs=(P(("groups", "expert"), None), P(("groups", "expert"), None)),
        check_vma=False,
    )
```

```python
import functools
import jax
import jax.numpy as jnp
from jax import lax
from jax.experimental import pallas as pl
from jax.experimental.pallas import tpu as pltpu
from jax.sharding import PartitionSpec as P


def expert_forward(inputs, gate_mat, up_mat, down_mat):
    gate_act = jnp.dot(inputs, gate_mat, preferred_element_type=jnp.float32)
    up_act = jnp.dot(inputs, up_mat, preferred_element_type=jnp.float32)
    sigmoid_gate = jax.nn.sigmoid(gate_act)
    hidden = (gate_act * sigmoid_gate * up_act).astype(jnp.bfloat16)
    output = jnp.dot(hidden, down_mat, preferred_element_type=jnp.float32).astype(jnp.bfloat16)
    return (output, gate_act, up_act)


def expert_backward(incoming, gate_act, up_act, gate_mat, up_mat, down_mat):
    against = (((1,), (1,)), ((), ()))
    hidden_grad = lax.dot_general(incoming, down_mat, against, preferred_element_type=jnp.float32)
    sigmoid_gate = jax.nn.sigmoid(gate_act)
    gate_grad = (
        hidden_grad * up_act * sigmoid_gate * (1.0 + gate_act * (1.0 - sigmoid_gate))
    ).astype(jnp.bfloat16)
    up_grad = (hidden_grad * gate_act * sigmoid_gate).astype(jnp.bfloat16)
    summed = lax.dot_general(gate_grad, gate_mat, against, preferred_element_type=jnp.float32)
    summed = summed + lax.dot_general(up_grad, up_mat, against, preferred_element_type=jnp.float32)
    return summed.astype(jnp.bfloat16)


def per_device(
    tokens, out_grad, cluster_ids, routes, route_weights, gate_weight, up_weight, down_weight
):
    model_width = tokens.shape[1]
    cent_rows = routes.shape[0]
    fanout = routes.shape[1]
    experts = lax.axis_size("expert")
    capacity = min(cent_rows, 2 * cent_rows * fanout // experts)
    member = (cluster_ids[:, None] == jnp.arange(cent_rows, dtype=jnp.int32)[None, :]).astype(
        jnp.bfloat16
    )
    counts = jnp.sum(member.astype(jnp.float32), axis=0)
    contract = (((0,), (0,)), ((), ()))
    centroid = (
        lax.dot_general(member, tokens, contract, preferred_element_type=jnp.float32)
        / counts[:, None]
    )
    grad_sum = lax.dot_general(member, out_grad, contract, preferred_element_type=jnp.float32)
    pair_ids = routes.reshape(-1)
    matches = (pair_ids[:, None] == jnp.arange(experts, dtype=jnp.int32)[None, :]).astype(jnp.int32)
    earlier = jnp.cumsum(matches, axis=0) - matches
    position = jnp.sum(earlier * matches, axis=1)
    slot_of = (pair_ids * capacity + position).reshape(cent_rows, fanout)
    slot_range = jnp.arange(experts * capacity, dtype=jnp.int32)
    placing = jnp.any(slot_of[None, :, :] == slot_range[:, None, None], axis=2).astype(jnp.bfloat16)
    send_cent = jnp.dot(placing, centroid.astype(jnp.bfloat16), preferred_element_type=jnp.float32)
    send_cent = send_cent.astype(jnp.bfloat16).reshape(experts, capacity, model_width)
    send_grad = jnp.dot(placing, grad_sum.astype(jnp.bfloat16), preferred_element_type=jnp.float32)
    send_grad = send_grad.astype(jnp.bfloat16).reshape(experts, capacity, model_width)
    gate_mat = gate_weight[0]
    up_mat = up_weight[0]
    down_mat = down_weight[0]
    arrived = lax.all_to_all(send_cent, "expert", split_axis=0, concat_axis=0, tiled=True)
    output, gate_act, up_act = expert_forward(
        arrived.reshape(-1, model_width), gate_mat, up_mat, down_mat
    )
    results = lax.all_to_all(
        output.reshape(experts, capacity, model_width),
        "expert",
        split_axis=0,
        concat_axis=0,
        tiled=True,
    )
    arrived_grad = lax.all_to_all(send_grad, "expert", split_axis=0, concat_axis=0, tiled=True)
    input_grad = expert_backward(
        arrived_grad.reshape(-1, model_width), gate_act, up_act, gate_mat, up_mat, down_mat
    )
    results_grad = lax.all_to_all(
        input_grad.reshape(experts, capacity, model_width),
        "expert",
        split_axis=0,
        concat_axis=0,
        tiled=True,
    )
    returned = results.reshape(-1, model_width)[slot_of]
    returned_grad = results_grad.reshape(-1, model_width)[slot_of]
    combined = jnp.sum(route_weights[:, :, None] * returned.astype(jnp.float32), axis=1)
    centroid_grad = (
        jnp.sum(route_weights[:, :, None] * returned_grad.astype(jnp.float32), axis=1) - grad_sum
    )
    layer_out = tokens.astype(jnp.float32) + jnp.take(combined - centroid, cluster_ids, axis=0)
    token_grad = out_grad.astype(jnp.float32) + jnp.take(
        centroid_grad / counts[:, None], cluster_ids, axis=0
    )
    return (layer_out, token_grad)


AGAINST = (((1,), (1,)), ((), ()))


def ring_layout(ring):
    half = ring // 2
    places = {0: 0}
    for hop in range(1, half):
        places[hop] = 2 * hop - 1
        places[-hop] = 2 * hop
    places[half] = ring - 1
    places[-half] = ring - 1
    return places


def exchange_kernel(
    experts,
    ids_ref,
    tokens_ref,
    out_grad_ref,
    routes_ref,
    route_weights_ref,
    gate_ref,
    up_ref,
    down_ref,
    delta_ref,
    delta_grad_ref,
    cent_all,
    grad_all,
    gate_up,
    down,
    gate_up_turned,
    down_turned,
    hidden,
    hidden_grads,
    part_cent,
    part_grad,
    twin_cent,
    twin_grad,
    outgoing,
    incoming,
    centroid_keep,
    grad_keep,
    weight_sems,
    gather_send,
    gather_recv,
    share_send,
    share_recv,
    twin_send,
    twin_recv,
    ring_send,
    ring_recv,
):
    fanout, rows = routes_ref.shape
    width = tokens_ref.shape[1]
    hidden_width = down.shape[0]
    ring = experts // 2
    half = ring // 2
    places = ring_layout(ring)
    gathered = (cent_all, grad_all)
    parts = (part_cent, part_grad)
    twins = (twin_cent, twin_grad)

    me = lax.axis_index("expert")
    core = me % 2
    chip = me // 2
    column = chip % 2
    height = chip // 2
    spot = height + column * (ring - 1 - 2 * height)

    def device_at(position):
        side = position // half
        level = position + side * (ring - 1 - 2 * position)
        return (level * 2 + side) * 2 + core

    neighbour = (device_at((spot + 1) % ring), device_at((spot + ring - 1) % ring))
    twin = chip * 2 + (1 - core)

    weight_copies = [
        pltpu.make_async_copy(
            gate_ref.at[0], gate_up.at[:, pl.ds(0, hidden_width)], weight_sems.at[0]
        ),
        pltpu.make_async_copy(
            up_ref.at[0], gate_up.at[:, pl.ds(hidden_width, hidden_width)], weight_sems.at[1]
        ),
        pltpu.make_async_copy(down_ref.at[0], down, weight_sems.at[2]),
    ]
    for number in (2, 0, 1):
        weight_copies[number].start()

    barrier = pltpu.get_barrier_semaphore()
    for other in (neighbour[0], neighbour[1], twin):
        pl.semaphore_signal(
            barrier, inc=1, device_id={"expert": other}, device_id_type=pl.DeviceIdType.MESH
        )

    def block(distance, which):
        return pl.ds((places[distance] * 2 + which) * rows, rows)

    members = (
        lax.broadcasted_iota(jnp.int32, (rows, ids_ref.shape[1]), 0) == ids_ref[...]
    ).astype(jnp.float32)
    counts = jnp.sum(members, axis=1, keepdims=True)
    members = members.astype(jnp.bfloat16)
    centroid = jnp.dot(members, tokens_ref[...], preferred_element_type=jnp.float32) / counts
    grad_sum = jnp.dot(members, out_grad_ref[...], preferred_element_type=jnp.float32)
    centroid_keep[...] = centroid
    grad_keep[...] = grad_sum
    cent_all[block(0, 0), pl.ds(0, width)] = centroid.astype(jnp.bfloat16)
    grad_all[block(0, 0), :] = grad_sum.astype(jnp.bfloat16)

    lanes = lax.broadcasted_iota(jnp.int32, (128, rows), 0)
    spread = jnp.zeros((128, rows), jnp.float32)
    for k in range(fanout):
        spread = spread + jnp.where(
            lanes % experts == routes_ref[k : k + 1, :], route_weights_ref[k : k + 1, :], 0.0
        )
    high = spread.astype(jnp.bfloat16).astype(jnp.float32)
    middle = (spread - high).astype(jnp.bfloat16).astype(jnp.float32)
    low = spread - high - middle
    pieces = jnp.where(lanes < experts, high, jnp.where(lanes < 2 * experts, middle, low))
    same = lax.broadcasted_iota(jnp.int32, (rows, rows), 0) == lax.broadcasted_iota(
        jnp.int32, (rows, rows), 1
    )
    pieces = lax.dot_general(
        same.astype(jnp.bfloat16),
        pieces.astype(jnp.bfloat16),
        AGAINST,
        preferred_element_type=jnp.float32,
    )
    cent_all[block(0, 0), pl.ds(width, 128)] = pieces.astype(jnp.bfloat16)

    def remote(source, target, send, recv, other):
        return pltpu.make_async_remote_copy(
            src_ref=source,
            dst_ref=target,
            send_sem=send,
            recv_sem=recv,
            device_id={"expert": other},
            device_id_type=pl.DeviceIdType.MESH,
        )

    def signed(way, distance):
        return -distance if way == 0 else distance

    def hops_of(kind, way):
        return half if kind == way else half - 1

    def gather_copy(kind, way, hop):
        return remote(
            gathered[kind].at[block(signed(way, hop - 1), 0), :],
            gathered[kind].at[block(signed(way, hop), 0), :],
            gather_send.at[kind, way, hop - 1],
            gather_recv.at[kind, way, hop - 1],
            neighbour[way],
        )

    def share_copy(kind, distance):
        return remote(
            gathered[kind].at[block(distance, 0), :],
            gathered[kind].at[block(distance, 1), :],
            share_send.at[kind, places[distance]],
            share_recv.at[kind, places[distance]],
            twin,
        )

    def twin_copy(kind, distance):
        return remote(
            parts[kind].at[block(distance, 1), :],
            twins[kind].at[pl.ds(places[distance] * rows, rows), :],
            twin_send.at[kind, places[distance]],
            twin_recv.at[kind, places[distance]],
            twin,
        )

    def ring_copy(kind, way, step):
        return remote(
            outgoing.at[kind, way, step - 1],
            incoming.at[kind, way, step - 1],
            ring_send.at[kind, way, step - 1],
            ring_recv.at[kind, way, step - 1],
            neighbour[way],
        )

    started = []

    def start(copy):
        copy.start()
        started.append(copy)

    pl.semaphore_wait(barrier, 3)
    for way in range(2):
        for kind in range(2):
            start(gather_copy(kind, way, 1))
    for kind in range(2):
        start(share_copy(kind, 0))

    tile = 256 if hidden_width % 256 == 0 else hidden_width
    wide = 256 if width % 256 == 0 else width

    def turn(source, target, first, last):
        across = source.shape[1] // tile

        def body(r, carry):
            lines = pl.ds(pl.multiple_of(r * tile, tile), tile)
            for c in range(across):
                columns = pl.ds(c * tile, tile)
                target[columns, lines] = source[lines, columns].T
            return carry

        lax.fori_loop(first, last, body, 0)

    def first_half(low, high):
        span = pl.ds(low, high - low)
        held = pl.ds(0, high - low)

        def inner(j, carry):
            columns = pl.ds(pl.multiple_of(j * tile, tile), tile)
            later = pl.ds(pl.multiple_of(hidden_width + j * tile, tile), tile)
            inputs = cent_all[span, pl.ds(0, width)]
            gate_act = jnp.dot(inputs, gate_up[:, columns], preferred_element_type=jnp.float32)
            up_act = jnp.dot(inputs, gate_up[:, later], preferred_element_type=jnp.float32)
            grads = jnp.dot(
                grad_all[span, :], down_turned[:, columns], preferred_element_type=jnp.float32
            )
            sigmoid_gate = jax.nn.sigmoid(gate_act)
            hidden[held, columns] = (gate_act * sigmoid_gate * up_act).astype(jnp.bfloat16)
            hidden_grads[held, columns] = (
                grads * up_act * sigmoid_gate * (1.0 + gate_act * (1.0 - sigmoid_gate))
            ).astype(jnp.bfloat16)
            hidden_grads[held, later] = (grads * gate_act * sigmoid_gate).astype(jnp.bfloat16)
            return carry

        lax.fori_loop(0, hidden_width // tile, inner, 0)

    def second_half(low, high, first, last):
        span = pl.ds(low, high - low)
        held = pl.ds(0, high - low)
        pieces = cent_all[span, pl.ds(width, 128)].astype(jnp.float32)
        lanes = lax.broadcasted_iota(jnp.int32, (high - low, 128), 1)
        own = (lanes % experts == me) & (lanes < 3 * experts)
        weight = jnp.sum(jnp.where(own, pieces, 0.0), axis=1, keepdims=True)

        def outer(t, carry):
            columns = pl.ds(pl.multiple_of(t * wide, wide), wide)
            output = jnp.dot(hidden[held, :], down[:, columns], preferred_element_type=jnp.float32)
            output = output.astype(jnp.bfloat16).astype(jnp.float32)
            part_cent[span, columns] = output * weight
            summed = jnp.dot(
                hidden_grads[held, :],
                gate_up_turned[:, columns],
                preferred_element_type=jnp.float32,
            )
            summed = summed.astype(jnp.bfloat16).astype(jnp.float32)
            part_grad[span, columns] = summed * weight
            return carry

        lax.fori_loop(first, last, outer, 0)

    def contribution(kind, distance):
        twin_copy(kind, distance).wait_recv()
        return (
            parts[kind][block(distance, 0), :]
            + twins[kind][pl.ds(places[distance] * rows, rows), :]
        )

    def toward(way, distance):
        return distance if way == 0 else -distance

    def send_first(kind, way):
        total = contribution(kind, toward(way, hops_of(kind, way)))
        outgoing[kind, way, 0] = total.astype(jnp.bfloat16)
        start(ring_copy(kind, way, 1))

    def pass_on(hop, kind):
        for way in range(2):
            if hop <= hops_of(kind, way):
                gather_copy(kind, way, hop).wait_recv()
                if hop < hops_of(kind, way):
                    start(gather_copy(kind, way, hop + 1))
                start(share_copy(kind, signed(way, hop)))

    def distances_of(hop):
        if hop == 0 or hop == half:
            return (hop,)
        return (hop, -hop)

    def wait_shares(hop):
        for kind in range(2):
            for distance in distances_of(hop):
                share_copy(kind, distance).wait_recv()

    def start_twins(hop):
        for distance in distances_of(hop):
            for kind in range(2):
                start(twin_copy(kind, distance))

    bands = width // tile
    tiles = width // wide
    early = (2 * (half - 2) + 1) * 2 * rows
    middle = early + 4 * rows
    final = middle + 2 * rows
    moves = [(hop, kind) for hop in range(1, half - 1) for kind in range(2)]
    weight_copies[2].wait()
    turn(down, down_turned, 0, hidden_width // tile)
    weight_copies[0].wait()
    weight_copies[1].wait()
    for number, move in enumerate(moves):
        pass_on(*move)
        turn(
            gate_up,
            gate_up_turned,
            number * bands // len(moves),
            (number + 1) * bands // len(moves),
        )
    for hop in range(half - 1):
        wait_shares(hop)
    first_half(0, early)
    pass_on(half - 1, 0)
    second_half(0, early, 0, tiles // 2)
    pass_on(half - 1, 1)
    second_half(0, early, tiles // 2, tiles)
    for hop in range(half - 1):
        start_twins(hop)
    wait_shares(half - 1)
    first_half(early, middle)
    second_half(early, middle, 0, tiles)
    start_twins(half - 1)
    for kind in range(2):
        pass_on(half, kind)
    wait_shares(half)
    first_half(middle, final)
    for kind in range(2):
        send_first(kind, 1 - kind)
    second_half(middle, final, 0, tiles)
    start_twins(half)

    for kind in range(2):
        send_first(kind, kind)
    totals = [contribution(kind, 0) for kind in range(2)]
    delta_ref[...] = totals[0] - centroid_keep[...]
    delta_grad_ref[...] = totals[1] - grad_keep[...]
    for step in range(1, half + 1):
        for kind in range(2):
            for way in (1 - kind, kind):
                hops = hops_of(kind, way)
                if step > hops:
                    continue
                ring_copy(kind, way, step).wait_recv()
                arrived = incoming[kind, way, step - 1].astype(jnp.float32)
                if step < hops:
                    total = arrived + contribution(kind, toward(way, hops - step))
                    outgoing[kind, way, step] = total.astype(jnp.bfloat16)
                    start(ring_copy(kind, way, step + 1))
                elif kind == 0:
                    delta_ref[...] += arrived
                else:
                    delta_grad_ref[...] += arrived
    delta_grad_ref[...] = delta_grad_ref[...] / counts
    for copy in started:
        copy.wait_send()


def decode_kernel(ids_ref, tokens_ref, out_grad_ref, delta_ref, delta_grad_ref, out_ref, grad_ref):
    rows = delta_ref.shape[0]
    lines = lax.broadcasted_iota(jnp.int32, (3 * rows, ids_ref.shape[1]), 0)
    members = (lines % rows == ids_ref[...]).astype(jnp.bfloat16)
    contract = (((0,), (0,)), ((), ()))

    def spread(table):
        high = table.astype(jnp.bfloat16)
        rest = table - high.astype(jnp.float32)
        middle = rest.astype(jnp.bfloat16)
        low = (rest - middle.astype(jnp.float32)).astype(jnp.bfloat16)
        stacked = jnp.concatenate([high, middle, low], axis=0)
        return lax.dot_general(members, stacked, contract, preferred_element_type=jnp.float32)

    out_ref[...] = tokens_ref[...].astype(jnp.float32) + spread(delta_ref[...])
    grad_ref[...] = out_grad_ref[...].astype(jnp.float32) + spread(delta_grad_ref[...])


def ring_per_device(
    tokens, out_grad, cluster_ids, routes, route_weights, gate_weight, up_weight, down_weight
):
    experts = lax.axis_size("expert")
    rows = routes.shape[0]
    count, width = tokens.shape
    hidden_width = gate_weight.shape[2]
    ring = experts // 2
    half = ring // 2
    held = experts * rows
    ids = cluster_ids.reshape(1, count)
    vmem = pl.BlockSpec(memory_space=pltpu.VMEM)
    anywhere = pl.BlockSpec(memory_space=pl.ANY)
    table = jax.ShapeDtypeStruct((rows, width), jnp.float32)
    bf16, f32, dma = jnp.bfloat16, jnp.float32, pltpu.SemaphoreType.DMA
    delta, delta_grad = pl.pallas_call(
        functools.partial(exchange_kernel, experts),
        out_shape=(table, table),
        in_specs=[vmem] * 5 + [anywhere] * 3,
        out_specs=(vmem, vmem),
        scratch_shapes=[
            pltpu.VMEM((held, width + 128), bf16),
            pltpu.VMEM((held, width), bf16),
            pltpu.VMEM((width, 2 * hidden_width), bf16),
            pltpu.VMEM((hidden_width, width), bf16),
            pltpu.VMEM((2 * hidden_width, width), bf16),
            pltpu.VMEM((width, hidden_width), bf16),
            pltpu.VMEM((held, hidden_width), bf16),
            pltpu.VMEM((held, 2 * hidden_width), bf16),
            pltpu.VMEM((held, width), f32),
            pltpu.VMEM((held, width), f32),
            pltpu.VMEM((ring * rows, width), f32),
            pltpu.VMEM((ring * rows, width), f32),
            pltpu.VMEM((2, 2, half, rows, width), bf16),
            pltpu.VMEM((2, 2, half, rows, width), bf16),
            pltpu.VMEM((rows, width), f32),
            pltpu.VMEM((rows, width), f32),
            dma((3,)),
            dma((2, 2, half)),
            dma((2, 2, half)),
            dma((2, ring)),
            dma((2, ring)),
            dma((2, ring)),
            dma((2, ring)),
            dma((2, 2, half)),
            dma((2, 2, half)),
        ],
        compiler_params=pltpu.CompilerParams(
            collective_id=0, has_side_effects=True, vmem_limit_bytes=56 * 1024 * 1024
        ),
        cost_estimate=pl.CostEstimate(
            flops=12 * held * width * hidden_width,
            bytes_accessed=6 * width * hidden_width,
            transcendentals=held * hidden_width,
        ),
    )(ids, tokens, out_grad, routes.T, route_weights.T, gate_weight, up_weight, down_weight)
    step = 512 if width % 512 == 0 else width
    whole = pl.BlockSpec((1, count), lambda i: (0, 0))
    tall = pl.BlockSpec((count, step), lambda i: (0, i))
    short = pl.BlockSpec((rows, step), lambda i: (0, i))
    result = jax.ShapeDtypeStruct((count, width), jnp.float32)
    return pl.pallas_call(
        decode_kernel,
        grid=(width // step,),
        out_shape=(result, result),
        in_specs=[whole, tall, tall, short, short],
        out_specs=(tall, tall),
    )(ids, tokens, out_grad, delta, delta_grad)


def solution(mesh):
    placed = (
        P(("groups", "expert"), None),
        P(("groups", "expert"), None),
        P(("groups", "expert")),
        P(("groups", "expert"), None),
        P(("groups", "expert"), None),
        P("expert", None, None),
        P("expert", None, None),
        P("expert", None, None),
    )
    size = mesh.shape["expert"]
    ringed = size % 4 == 0 and 12 <= size <= 32
    return jax.shard_map(
        ring_per_device if ringed else per_device,
        mesh=mesh,
        in_specs=placed,
        out_specs=(P(("groups", "expert"), None), P(("groups", "expert"), None)),
        check_vma=False,
    )
```

```python
import functools
import jax
import jax.numpy as jnp
from jax import lax
from jax.experimental import pallas as pl
from jax.experimental.pallas import tpu as pltpu
from jax.sharding import PartitionSpec as P


def expert_forward(inputs, gate_mat, up_mat, down_mat):
    gate_act = jnp.dot(inputs, gate_mat, preferred_element_type=jnp.float32)
    up_act = jnp.dot(inputs, up_mat, preferred_element_type=jnp.float32)
    sigmoid_gate = jax.nn.sigmoid(gate_act)
    hidden = (gate_act * sigmoid_gate * up_act).astype(jnp.bfloat16)
    output = jnp.dot(hidden, down_mat, preferred_element_type=jnp.float32).astype(jnp.bfloat16)
    return (output, gate_act, up_act)


def expert_backward(incoming, gate_act, up_act, gate_mat, up_mat, down_mat):
    against = (((1,), (1,)), ((), ()))
    hidden_grad = lax.dot_general(incoming, down_mat, against, preferred_element_type=jnp.float32)
    sigmoid_gate = jax.nn.sigmoid(gate_act)
    gate_grad = (
        hidden_grad * up_act * sigmoid_gate * (1.0 + gate_act * (1.0 - sigmoid_gate))
    ).astype(jnp.bfloat16)
    up_grad = (hidden_grad * gate_act * sigmoid_gate).astype(jnp.bfloat16)
    summed = lax.dot_general(gate_grad, gate_mat, against, preferred_element_type=jnp.float32)
    summed = summed + lax.dot_general(up_grad, up_mat, against, preferred_element_type=jnp.float32)
    return summed.astype(jnp.bfloat16)


def per_device(
    tokens, out_grad, cluster_ids, routes, route_weights, gate_weight, up_weight, down_weight
):
    model_width = tokens.shape[1]
    cent_rows = routes.shape[0]
    fanout = routes.shape[1]
    experts = lax.axis_size("expert")
    capacity = min(cent_rows, 2 * cent_rows * fanout // experts)
    member = (cluster_ids[:, None] == jnp.arange(cent_rows, dtype=jnp.int32)[None, :]).astype(
        jnp.bfloat16
    )
    counts = jnp.sum(member.astype(jnp.float32), axis=0)
    contract = (((0,), (0,)), ((), ()))
    centroid = (
        lax.dot_general(member, tokens, contract, preferred_element_type=jnp.float32)
        / counts[:, None]
    )
    grad_sum = lax.dot_general(member, out_grad, contract, preferred_element_type=jnp.float32)
    pair_ids = routes.reshape(-1)
    matches = (pair_ids[:, None] == jnp.arange(experts, dtype=jnp.int32)[None, :]).astype(jnp.int32)
    earlier = jnp.cumsum(matches, axis=0) - matches
    position = jnp.sum(earlier * matches, axis=1)
    slot_of = (pair_ids * capacity + position).reshape(cent_rows, fanout)
    slot_range = jnp.arange(experts * capacity, dtype=jnp.int32)
    placing = jnp.any(slot_of[None, :, :] == slot_range[:, None, None], axis=2).astype(jnp.bfloat16)
    send_cent = jnp.dot(placing, centroid.astype(jnp.bfloat16), preferred_element_type=jnp.float32)
    send_cent = send_cent.astype(jnp.bfloat16).reshape(experts, capacity, model_width)
    send_grad = jnp.dot(placing, grad_sum.astype(jnp.bfloat16), preferred_element_type=jnp.float32)
    send_grad = send_grad.astype(jnp.bfloat16).reshape(experts, capacity, model_width)
    gate_mat = gate_weight[0]
    up_mat = up_weight[0]
    down_mat = down_weight[0]
    arrived = lax.all_to_all(send_cent, "expert", split_axis=0, concat_axis=0, tiled=True)
    output, gate_act, up_act = expert_forward(
        arrived.reshape(-1, model_width), gate_mat, up_mat, down_mat
    )
    results = lax.all_to_all(
        output.reshape(experts, capacity, model_width),
        "expert",
        split_axis=0,
        concat_axis=0,
        tiled=True,
    )
    arrived_grad = lax.all_to_all(send_grad, "expert", split_axis=0, concat_axis=0, tiled=True)
    input_grad = expert_backward(
        arrived_grad.reshape(-1, model_width), gate_act, up_act, gate_mat, up_mat, down_mat
    )
    results_grad = lax.all_to_all(
        input_grad.reshape(experts, capacity, model_width),
        "expert",
        split_axis=0,
        concat_axis=0,
        tiled=True,
    )
    returned = results.reshape(-1, model_width)[slot_of]
    returned_grad = results_grad.reshape(-1, model_width)[slot_of]
    combined = jnp.sum(route_weights[:, :, None] * returned.astype(jnp.float32), axis=1)
    centroid_grad = (
        jnp.sum(route_weights[:, :, None] * returned_grad.astype(jnp.float32), axis=1) - grad_sum
    )
    layer_out = tokens.astype(jnp.float32) + jnp.take(combined - centroid, cluster_ids, axis=0)
    token_grad = out_grad.astype(jnp.float32) + jnp.take(
        centroid_grad / counts[:, None], cluster_ids, axis=0
    )
    return (layer_out, token_grad)


AGAINST = (((1,), (1,)), ((), ()))


def ring_layout(ring):
    half = ring // 2
    places = {0: 0}
    for hop in range(1, half):
        places[hop] = 2 * hop - 1
        places[-hop] = 2 * hop
    places[half] = ring - 1
    places[-half] = ring - 1
    return places


def exchange_kernel(
    experts,
    ids_ref,
    tokens_ref,
    out_grad_ref,
    routes_ref,
    route_weights_ref,
    gate_ref,
    up_ref,
    down_ref,
    delta_ref,
    delta_grad_ref,
    cent_all,
    grad_all,
    gate_up,
    down,
    gate_up_turned,
    down_turned,
    hidden,
    hidden_grads,
    part_cent,
    part_grad,
    twin_cent,
    twin_grad,
    outgoing,
    incoming,
    centroid_keep,
    grad_keep,
    weight_sems,
    gather_send,
    gather_recv,
    share_send,
    share_recv,
    twin_send,
    twin_recv,
    ring_send,
    ring_recv,
):
    fanout, rows = routes_ref.shape
    width = tokens_ref.shape[1]
    hidden_width = down.shape[0]
    ring = experts // 2
    half = ring // 2
    places = ring_layout(ring)
    gathered = (cent_all, grad_all)
    parts = (part_cent, part_grad)
    twins = (twin_cent, twin_grad)

    me = lax.axis_index("expert")
    core = me % 2
    chip = me // 2
    column = chip % 2
    height = chip // 2
    spot = height + column * (ring - 1 - 2 * height)

    def device_at(position):
        side = position // half
        level = position + side * (ring - 1 - 2 * position)
        return (level * 2 + side) * 2 + core

    neighbour = (device_at((spot + 1) % ring), device_at((spot + ring - 1) % ring))
    twin = chip * 2 + (1 - core)

    weight_copies = [
        pltpu.make_async_copy(
            gate_ref.at[0], gate_up.at[:, pl.ds(0, hidden_width)], weight_sems.at[0]
        ),
        pltpu.make_async_copy(
            up_ref.at[0], gate_up.at[:, pl.ds(hidden_width, hidden_width)], weight_sems.at[1]
        ),
        pltpu.make_async_copy(down_ref.at[0], down, weight_sems.at[2]),
    ]
    for number in (2, 0, 1):
        weight_copies[number].start()

    barrier = pltpu.get_barrier_semaphore()
    for other in (neighbour[0], neighbour[1], twin):
        pl.semaphore_signal(
            barrier, inc=1, device_id={"expert": other}, device_id_type=pl.DeviceIdType.MESH
        )

    def block(distance, which):
        return pl.ds((places[distance] * 2 + which) * rows, rows)

    members = (
        lax.broadcasted_iota(jnp.int32, (rows, ids_ref.shape[1]), 0) == ids_ref[...]
    ).astype(jnp.float32)
    counts = jnp.sum(members, axis=1, keepdims=True)
    members = members.astype(jnp.bfloat16)
    centroid = jnp.dot(members, tokens_ref[...], preferred_element_type=jnp.float32) / counts
    grad_sum = jnp.dot(members, out_grad_ref[...], preferred_element_type=jnp.float32)
    centroid_keep[...] = centroid
    grad_keep[...] = grad_sum
    cent_all[block(0, 0), pl.ds(0, width)] = centroid.astype(jnp.bfloat16)
    grad_all[block(0, 0), :] = grad_sum.astype(jnp.bfloat16)

    lanes = lax.broadcasted_iota(jnp.int32, (128, rows), 0)
    spread = jnp.zeros((128, rows), jnp.float32)
    for k in range(fanout):
        spread = spread + jnp.where(
            lanes % experts == routes_ref[k : k + 1, :], route_weights_ref[k : k + 1, :], 0.0
        )
    high = spread.astype(jnp.bfloat16).astype(jnp.float32)
    middle = (spread - high).astype(jnp.bfloat16).astype(jnp.float32)
    low = spread - high - middle
    pieces = jnp.where(lanes < experts, high, jnp.where(lanes < 2 * experts, middle, low))
    same = lax.broadcasted_iota(jnp.int32, (rows, rows), 0) == lax.broadcasted_iota(
        jnp.int32, (rows, rows), 1
    )
    pieces = lax.dot_general(
        same.astype(jnp.bfloat16),
        pieces.astype(jnp.bfloat16),
        AGAINST,
        preferred_element_type=jnp.float32,
    )
    cent_all[block(0, 0), pl.ds(width, 128)] = pieces.astype(jnp.bfloat16)

    def remote(source, target, send, recv, other):
        return pltpu.make_async_remote_copy(
            src_ref=source,
            dst_ref=target,
            send_sem=send,
            recv_sem=recv,
            device_id={"expert": other},
            device_id_type=pl.DeviceIdType.MESH,
        )

    def signed(way, distance):
        return -distance if way == 0 else distance

    def hops_of(kind, way):
        return half if kind == way else half - 1

    def gather_copy(kind, way, hop):
        return remote(
            gathered[kind].at[block(signed(way, hop - 1), 0), :],
            gathered[kind].at[block(signed(way, hop), 0), :],
            gather_send.at[kind, way, hop - 1],
            gather_recv.at[kind, way, hop - 1],
            neighbour[way],
        )

    def share_copy(kind, distance):
        return remote(
            gathered[kind].at[block(distance, 0), :],
            gathered[kind].at[block(distance, 1), :],
            share_send.at[kind, places[distance]],
            share_recv.at[kind, places[distance]],
            twin,
        )

    def twin_copy(kind, distance):
        return remote(
            parts[kind].at[block(distance, 1), :],
            twins[kind].at[pl.ds(places[distance] * rows, rows), :],
            twin_send.at[kind, places[distance]],
            twin_recv.at[kind, places[distance]],
            twin,
        )

    def ring_copy(kind, way, step):
        return remote(
            outgoing.at[kind, way, step - 1],
            incoming.at[kind, way, step - 1],
            ring_send.at[kind, way, step - 1],
            ring_recv.at[kind, way, step - 1],
            neighbour[way],
        )

    started = []

    def start(copy):
        copy.start()
        started.append(copy)

    pl.semaphore_wait(barrier, 3)
    for way in range(2):
        for kind in range(2):
            start(gather_copy(kind, way, 1))
    for kind in range(2):
        start(share_copy(kind, 0))

    tile = 256 if hidden_width % 256 == 0 else hidden_width
    wide = width // 2

    def turn(source, target, first, last):
        across = source.shape[1] // tile

        def body(r, carry):
            lines = pl.ds(pl.multiple_of(r * tile, tile), tile)
            for c in range(across):
                columns = pl.ds(c * tile, tile)
                target[columns, lines] = source[lines, columns].T
            return carry

        lax.fori_loop(first, last, body, 0)

    def first_half(low, high):
        span = pl.ds(low, high - low)
        held = pl.ds(0, high - low)

        acts = jnp.dot(
            cent_all[span, pl.ds(0, width)], gate_up[...], preferred_element_type=jnp.float32
        )
        grads = jnp.dot(grad_all[span, :], down_turned[...], preferred_element_type=jnp.float32)
        gate_act = acts[:, :hidden_width]
        up_act = acts[:, hidden_width:]
        sigmoid_gate = jax.nn.sigmoid(gate_act)
        hidden[held, :] = (gate_act * sigmoid_gate * up_act).astype(jnp.bfloat16)
        hidden_grads[held, pl.ds(0, hidden_width)] = (
            grads * up_act * sigmoid_gate * (1.0 + gate_act * (1.0 - sigmoid_gate))
        ).astype(jnp.bfloat16)
        hidden_grads[held, pl.ds(hidden_width, hidden_width)] = (
            grads * gate_act * sigmoid_gate
        ).astype(jnp.bfloat16)

    def second_half(low, high):
        span = pl.ds(low, high - low)
        held = pl.ds(0, high - low)
        pieces = cent_all[span, pl.ds(width, 128)].astype(jnp.float32)
        lanes = lax.broadcasted_iota(jnp.int32, (high - low, 128), 1)
        own = (lanes % experts == me) & (lanes < 3 * experts)
        weight = jnp.sum(jnp.where(own, pieces, 0.0), axis=1, keepdims=True)

        for t in range(2):
            columns = pl.ds(t * wide, wide)
            output = jnp.dot(hidden[held, :], down[:, columns], preferred_element_type=jnp.float32)
            output = output.astype(jnp.bfloat16).astype(jnp.float32)
            part_cent[span, columns] = output * weight
            summed = jnp.dot(
                hidden_grads[held, :],
                gate_up_turned[:, columns],
                preferred_element_type=jnp.float32,
            )
            summed = summed.astype(jnp.bfloat16).astype(jnp.float32)
            part_grad[span, columns] = summed * weight

    def contribution(kind, distance):
        twin_copy(kind, distance).wait_recv()
        return (
            parts[kind][block(distance, 0), :]
            + twins[kind][pl.ds(places[distance] * rows, rows), :]
        )

    def toward(way, distance):
        return distance if way == 0 else -distance

    def send_first(kind, way):
        total = contribution(kind, toward(way, hops_of(kind, way)))
        outgoing[kind, way, 0] = total.astype(jnp.bfloat16)
        start(ring_copy(kind, way, 1))

    def pass_on(hop, kind):
        for way in range(2):
            if hop <= hops_of(kind, way):
                gather_copy(kind, way, hop).wait_recv()
                if hop < hops_of(kind, way):
                    start(gather_copy(kind, way, hop + 1))
                start(share_copy(kind, signed(way, hop)))

    def distances_of(hop):
        if hop == 0 or hop == half:
            return (hop,)
        return (hop, -hop)

    def wait_shares(hop):
        for kind in range(2):
            for distance in distances_of(hop):
                share_copy(kind, distance).wait_recv()

    def start_twins(hop):
        for distance in distances_of(hop):
            for kind in range(2):
                start(twin_copy(kind, distance))

    bands = width // tile
    weight_copies[2].wait()
    turn(down, down_turned, 0, hidden_width // tile)
    pass_on(1, 0)
    weight_copies[0].wait()
    weight_copies[1].wait()
    turn(gate_up, gate_up_turned, 0, bands // 2)
    pass_on(1, 1)
    turn(gate_up, gate_up_turned, bands // 2, bands)
    low = 0
    for hop in range(1, half + 1):
        included = (0, 1) if hop == 1 else (hop,)
        high = low + sum(len(distances_of(each)) for each in included) * 2 * rows
        if hop < half:
            pass_on(hop + 1, 0)
        for each in included:
            wait_shares(each)
        first_half(low, high)
        if hop < half:
            pass_on(hop + 1, 1)
        else:
            for kind in range(2):
                send_first(kind, 1 - kind)
        second_half(low, high)
        for each in included:
            start_twins(each)
        low = high

    for kind in range(2):
        send_first(kind, kind)
    totals = [contribution(kind, 0) for kind in range(2)]
    delta_ref[...] = totals[0] - centroid_keep[...]
    delta_grad_ref[...] = totals[1] - grad_keep[...]
    for step in range(1, half + 1):
        for kind in range(2):
            for way in (1 - kind, kind):
                hops = hops_of(kind, way)
                if step > hops:
                    continue
                ring_copy(kind, way, step).wait_recv()
                arrived = incoming[kind, way, step - 1].astype(jnp.float32)
                if step < hops:
                    total = arrived + contribution(kind, toward(way, hops - step))
                    outgoing[kind, way, step] = total.astype(jnp.bfloat16)
                    start(ring_copy(kind, way, step + 1))
                elif kind == 0:
                    delta_ref[...] += arrived
                else:
                    delta_grad_ref[...] += arrived
    delta_grad_ref[...] = delta_grad_ref[...] / counts
    for copy in started:
        copy.wait_send()


def decode_kernel(ids_ref, tokens_ref, out_grad_ref, delta_ref, delta_grad_ref, out_ref, grad_ref):
    rows = delta_ref.shape[0]
    lines = lax.broadcasted_iota(jnp.int32, (3 * rows, ids_ref.shape[1]), 0)
    members = (lines % rows == ids_ref[...]).astype(jnp.bfloat16)
    contract = (((0,), (0,)), ((), ()))

    def spread(table):
        high = table.astype(jnp.bfloat16)
        rest = table - high.astype(jnp.float32)
        middle = rest.astype(jnp.bfloat16)
        low = (rest - middle.astype(jnp.float32)).astype(jnp.bfloat16)
        stacked = jnp.concatenate([high, middle, low], axis=0)
        return lax.dot_general(members, stacked, contract, preferred_element_type=jnp.float32)

    out_ref[...] = tokens_ref[...].astype(jnp.float32) + spread(delta_ref[...])
    grad_ref[...] = out_grad_ref[...].astype(jnp.float32) + spread(delta_grad_ref[...])


def ring_per_device(
    tokens, out_grad, cluster_ids, routes, route_weights, gate_weight, up_weight, down_weight
):
    experts = lax.axis_size("expert")
    rows = routes.shape[0]
    count, width = tokens.shape
    hidden_width = gate_weight.shape[2]
    ring = experts // 2
    half = ring // 2
    held = experts * rows
    ids = cluster_ids.reshape(1, count)
    vmem = pl.BlockSpec(memory_space=pltpu.VMEM)
    anywhere = pl.BlockSpec(memory_space=pl.ANY)
    table = jax.ShapeDtypeStruct((rows, width), jnp.float32)
    bf16, f32, dma = jnp.bfloat16, jnp.float32, pltpu.SemaphoreType.DMA
    delta, delta_grad = pl.pallas_call(
        functools.partial(exchange_kernel, experts),
        out_shape=(table, table),
        in_specs=[vmem] * 5 + [anywhere] * 3,
        out_specs=(vmem, vmem),
        scratch_shapes=[
            pltpu.VMEM((held, width + 128), bf16),
            pltpu.VMEM((held, width), bf16),
            pltpu.VMEM((width, 2 * hidden_width), bf16),
            pltpu.VMEM((hidden_width, width), bf16),
            pltpu.VMEM((2 * hidden_width, width), bf16),
            pltpu.VMEM((width, hidden_width), bf16),
            pltpu.VMEM((6 * rows, hidden_width), bf16),
            pltpu.VMEM((6 * rows, 2 * hidden_width), bf16),
            pltpu.VMEM((held, width), f32),
            pltpu.VMEM((held, width), f32),
            pltpu.VMEM((ring * rows, width), f32),
            pltpu.VMEM((ring * rows, width), f32),
            pltpu.VMEM((2, 2, half, rows, width), bf16),
            pltpu.VMEM((2, 2, half, rows, width), bf16),
            pltpu.VMEM((rows, width), f32),
            pltpu.VMEM((rows, width), f32),
            dma((3,)),
            dma((2, 2, half)),
            dma((2, 2, half)),
            dma((2, ring)),
            dma((2, ring)),
            dma((2, ring)),
            dma((2, ring)),
            dma((2, 2, half)),
            dma((2, 2, half)),
        ],
        compiler_params=pltpu.CompilerParams(
            collective_id=0, has_side_effects=True, vmem_limit_bytes=56 * 1024 * 1024
        ),
        cost_estimate=pl.CostEstimate(
            flops=12 * held * width * hidden_width,
            bytes_accessed=6 * width * hidden_width,
            transcendentals=held * hidden_width,
        ),
    )(ids, tokens, out_grad, routes.T, route_weights.T, gate_weight, up_weight, down_weight)
    step = 512 if width % 512 == 0 else width
    whole = pl.BlockSpec((1, count), lambda i: (0, 0))
    tall = pl.BlockSpec((count, step), lambda i: (0, i))
    short = pl.BlockSpec((rows, step), lambda i: (0, i))
    result = jax.ShapeDtypeStruct((count, width), jnp.float32)
    return pl.pallas_call(
        decode_kernel,
        grid=(width // step,),
        out_shape=(result, result),
        in_specs=[whole, tall, tall, short, short],
        out_specs=(tall, tall),
    )(ids, tokens, out_grad, delta, delta_grad)


def solution(mesh):
    placed = (
        P(("groups", "expert"), None),
        P(("groups", "expert"), None),
        P(("groups", "expert")),
        P(("groups", "expert"), None),
        P(("groups", "expert"), None),
        P("expert", None, None),
        P("expert", None, None),
        P("expert", None, None),
    )
    size = mesh.shape["expert"]
    ringed = size % 4 == 0 and 12 <= size <= 32
    return jax.shard_map(
        ring_per_device if ringed else per_device,
        mesh=mesh,
        in_specs=placed,
        out_specs=(P(("groups", "expert"), None), P(("groups", "expert"), None)),
        check_vma=False,
    )
```

```python
import functools
import jax
import jax.numpy as jnp
from jax import lax
from jax.experimental import pallas as pl
from jax.experimental.pallas import tpu as pltpu
from jax.sharding import PartitionSpec as P


def expert_forward(inputs, gate_mat, up_mat, down_mat):
    gate_act = jnp.dot(inputs, gate_mat, preferred_element_type=jnp.float32)
    up_act = jnp.dot(inputs, up_mat, preferred_element_type=jnp.float32)
    sigmoid_gate = jax.nn.sigmoid(gate_act)
    hidden = (gate_act * sigmoid_gate * up_act).astype(jnp.bfloat16)
    output = jnp.dot(hidden, down_mat, preferred_element_type=jnp.float32).astype(jnp.bfloat16)
    return (output, gate_act, up_act)


def expert_backward(incoming, gate_act, up_act, gate_mat, up_mat, down_mat):
    against = (((1,), (1,)), ((), ()))
    hidden_grad = lax.dot_general(incoming, down_mat, against, preferred_element_type=jnp.float32)
    sigmoid_gate = jax.nn.sigmoid(gate_act)
    gate_grad = (
        hidden_grad * up_act * sigmoid_gate * (1.0 + gate_act * (1.0 - sigmoid_gate))
    ).astype(jnp.bfloat16)
    up_grad = (hidden_grad * gate_act * sigmoid_gate).astype(jnp.bfloat16)
    summed = lax.dot_general(gate_grad, gate_mat, against, preferred_element_type=jnp.float32)
    summed = summed + lax.dot_general(up_grad, up_mat, against, preferred_element_type=jnp.float32)
    return summed.astype(jnp.bfloat16)


def per_device(
    tokens, out_grad, cluster_ids, routes, route_weights, gate_weight, up_weight, down_weight
):
    model_width = tokens.shape[1]
    cent_rows = routes.shape[0]
    fanout = routes.shape[1]
    experts = lax.axis_size("expert")
    capacity = min(cent_rows, 2 * cent_rows * fanout // experts)
    member = (cluster_ids[:, None] == jnp.arange(cent_rows, dtype=jnp.int32)[None, :]).astype(
        jnp.bfloat16
    )
    counts = jnp.sum(member.astype(jnp.float32), axis=0)
    contract = (((0,), (0,)), ((), ()))
    centroid = (
        lax.dot_general(member, tokens, contract, preferred_element_type=jnp.float32)
        / counts[:, None]
    )
    grad_sum = lax.dot_general(member, out_grad, contract, preferred_element_type=jnp.float32)
    pair_ids = routes.reshape(-1)
    matches = (pair_ids[:, None] == jnp.arange(experts, dtype=jnp.int32)[None, :]).astype(jnp.int32)
    earlier = jnp.cumsum(matches, axis=0) - matches
    position = jnp.sum(earlier * matches, axis=1)
    slot_of = (pair_ids * capacity + position).reshape(cent_rows, fanout)
    slot_range = jnp.arange(experts * capacity, dtype=jnp.int32)
    placing = jnp.any(slot_of[None, :, :] == slot_range[:, None, None], axis=2).astype(jnp.bfloat16)
    send_cent = jnp.dot(placing, centroid.astype(jnp.bfloat16), preferred_element_type=jnp.float32)
    send_cent = send_cent.astype(jnp.bfloat16).reshape(experts, capacity, model_width)
    send_grad = jnp.dot(placing, grad_sum.astype(jnp.bfloat16), preferred_element_type=jnp.float32)
    send_grad = send_grad.astype(jnp.bfloat16).reshape(experts, capacity, model_width)
    gate_mat = gate_weight[0]
    up_mat = up_weight[0]
    down_mat = down_weight[0]
    arrived = lax.all_to_all(send_cent, "expert", split_axis=0, concat_axis=0, tiled=True)
    output, gate_act, up_act = expert_forward(
        arrived.reshape(-1, model_width), gate_mat, up_mat, down_mat
    )
    results = lax.all_to_all(
        output.reshape(experts, capacity, model_width),
        "expert",
        split_axis=0,
        concat_axis=0,
        tiled=True,
    )
    arrived_grad = lax.all_to_all(send_grad, "expert", split_axis=0, concat_axis=0, tiled=True)
    input_grad = expert_backward(
        arrived_grad.reshape(-1, model_width), gate_act, up_act, gate_mat, up_mat, down_mat
    )
    results_grad = lax.all_to_all(
        input_grad.reshape(experts, capacity, model_width),
        "expert",
        split_axis=0,
        concat_axis=0,
        tiled=True,
    )
    returned = results.reshape(-1, model_width)[slot_of]
    returned_grad = results_grad.reshape(-1, model_width)[slot_of]
    combined = jnp.sum(route_weights[:, :, None] * returned.astype(jnp.float32), axis=1)
    centroid_grad = (
        jnp.sum(route_weights[:, :, None] * returned_grad.astype(jnp.float32), axis=1) - grad_sum
    )
    layer_out = tokens.astype(jnp.float32) + jnp.take(combined - centroid, cluster_ids, axis=0)
    token_grad = out_grad.astype(jnp.float32) + jnp.take(
        centroid_grad / counts[:, None], cluster_ids, axis=0
    )
    return (layer_out, token_grad)


AGAINST = (((1,), (1,)), ((), ()))


def ring_layout(ring):
    half = ring // 2
    places = {0: 0}
    for hop in range(1, half):
        places[hop] = 2 * hop - 1
        places[-hop] = 2 * hop
    places[half] = ring - 1
    places[-half] = ring - 1
    return places


def exchange_kernel(
    experts,
    ids_ref,
    tokens_ref,
    out_grad_ref,
    routes_ref,
    route_weights_ref,
    gate_ref,
    up_ref,
    down_ref,
    delta_ref,
    delta_grad_ref,
    cent_all,
    grad_all,
    gate_up,
    down,
    gate_up_turned,
    down_turned,
    hidden,
    hidden_grads,
    part_cent,
    part_grad,
    twin_cent,
    twin_grad,
    outgoing,
    incoming,
    centroid_keep,
    grad_keep,
    weight_sems,
    gather_send,
    gather_recv,
    share_send,
    share_recv,
    twin_send,
    twin_recv,
    ring_send,
    ring_recv,
):
    fanout, rows = routes_ref.shape
    width = tokens_ref.shape[1]
    hidden_width = down.shape[0]
    ring = experts // 2
    half = ring // 2
    wide = width // 2
    places = ring_layout(ring)
    gathered = (cent_all, grad_all)
    parts = (part_cent, part_grad)
    twins = (twin_cent, twin_grad)

    me = lax.axis_index("expert")
    core = me % 2
    chip = me // 2
    column = chip % 2
    height = chip // 2
    spot = height + column * (ring - 1 - 2 * height)

    def device_at(position):
        side = position // half
        level = position + side * (ring - 1 - 2 * position)
        return (level * 2 + side) * 2 + core

    neighbour = (device_at((spot + 1) % ring), device_at((spot + ring - 1) % ring))
    twin = chip * 2 + (1 - core)

    weight_copies = [
        pltpu.make_async_copy(
            gate_ref.at[0], gate_up.at[:, pl.ds(0, hidden_width)], weight_sems.at[0]
        ),
        pltpu.make_async_copy(
            up_ref.at[0], gate_up.at[:, pl.ds(hidden_width, hidden_width)], weight_sems.at[1]
        ),
        pltpu.make_async_copy(down_ref.at[0], down, weight_sems.at[2]),
    ]
    for number in (2, 0, 1):
        weight_copies[number].start()

    barrier = pltpu.get_barrier_semaphore()
    for other in (neighbour[0], neighbour[1], twin):
        pl.semaphore_signal(
            barrier, inc=1, device_id={"expert": other}, device_id_type=pl.DeviceIdType.MESH
        )

    def block(distance, which):
        return pl.ds((places[distance] * 2 + which) * rows, rows)

    members = (
        lax.broadcasted_iota(jnp.int32, (rows, ids_ref.shape[1]), 0) == ids_ref[...]
    ).astype(jnp.float32)
    counts = jnp.sum(members, axis=1, keepdims=True)
    members = members.astype(jnp.bfloat16)
    centroid = jnp.dot(members, tokens_ref[...], preferred_element_type=jnp.float32) / counts
    grad_sum = jnp.dot(members, out_grad_ref[...], preferred_element_type=jnp.float32)
    centroid_keep[...] = centroid
    grad_keep[...] = grad_sum
    cent_all[block(0, 0), pl.ds(0, width)] = centroid.astype(jnp.bfloat16)
    grad_all[block(0, 0), :] = grad_sum.astype(jnp.bfloat16)

    lanes = lax.broadcasted_iota(jnp.int32, (128, rows), 0)
    spread = jnp.zeros((128, rows), jnp.float32)
    for k in range(fanout):
        spread = spread + jnp.where(
            lanes % experts == routes_ref[k : k + 1, :], route_weights_ref[k : k + 1, :], 0.0
        )
    high = spread.astype(jnp.bfloat16).astype(jnp.float32)
    middle = (spread - high).astype(jnp.bfloat16).astype(jnp.float32)
    low = spread - high - middle
    pieces = jnp.where(lanes < experts, high, jnp.where(lanes < 2 * experts, middle, low))
    same = lax.broadcasted_iota(jnp.int32, (rows, rows), 0) == lax.broadcasted_iota(
        jnp.int32, (rows, rows), 1
    )
    pieces = lax.dot_general(
        same.astype(jnp.bfloat16),
        pieces.astype(jnp.bfloat16),
        AGAINST,
        preferred_element_type=jnp.float32,
    )
    cent_all[block(0, 0), pl.ds(width, 128)] = pieces.astype(jnp.bfloat16)

    def remote(source, target, send, recv, other):
        return pltpu.make_async_remote_copy(
            src_ref=source,
            dst_ref=target,
            send_sem=send,
            recv_sem=recv,
            device_id={"expert": other},
            device_id_type=pl.DeviceIdType.MESH,
        )

    def signed(way, distance):
        return -distance if way == 0 else distance

    def hops_of(kind, way):
        return half if kind == way else half - 1

    def gather_copy(kind, way, hop):
        return remote(
            gathered[kind].at[block(signed(way, hop - 1), 0), :],
            gathered[kind].at[block(signed(way, hop), 0), :],
            gather_send.at[kind, way, hop - 1],
            gather_recv.at[kind, way, hop - 1],
            neighbour[way],
        )

    def share_copy(kind, distance):
        return remote(
            gathered[kind].at[block(distance, 0), :],
            gathered[kind].at[block(distance, 1), :],
            share_send.at[kind, places[distance]],
            share_recv.at[kind, places[distance]],
            twin,
        )

    def twin_copy(kind, distance, piece):
        columns = pl.ds(piece * wide, wide)
        return remote(
            parts[kind].at[block(distance, 1), columns],
            twins[kind].at[pl.ds(places[distance] * rows, rows), columns],
            twin_send.at[kind, places[distance], piece],
            twin_recv.at[kind, places[distance], piece],
            twin,
        )

    def ring_copy(kind, way, step, piece):
        return remote(
            outgoing.at[kind, way, step - 1, piece],
            incoming.at[kind, way, step - 1, piece],
            ring_send.at[kind, way, step - 1, piece],
            ring_recv.at[kind, way, step - 1, piece],
            neighbour[way],
        )

    started = []

    def start(copy):
        copy.start()
        started.append(copy)

    pl.semaphore_wait(barrier, 3)
    for way in range(2):
        for kind in range(2):
            start(gather_copy(kind, way, 1))
    for kind in range(2):
        start(share_copy(kind, 0))

    tile = 256 if hidden_width % 256 == 0 else hidden_width

    def turn(source, target, first, last):
        across = source.shape[1] // tile

        def body(r, carry):
            lines = pl.ds(pl.multiple_of(r * tile, tile), tile)
            for c in range(across):
                columns = pl.ds(c * tile, tile)
                target[columns, lines] = source[lines, columns].T
            return carry

        lax.fori_loop(first, last, body, 0)

    def first_half(low, high):
        span = pl.ds(low, high - low)
        held = pl.ds(0, high - low)

        acts = jnp.dot(
            cent_all[span, pl.ds(0, width)], gate_up[...], preferred_element_type=jnp.float32
        )
        grads = jnp.dot(grad_all[span, :], down_turned[...], preferred_element_type=jnp.float32)
        gate_act = acts[:, :hidden_width]
        up_act = acts[:, hidden_width:]
        sigmoid_gate = jax.nn.sigmoid(gate_act)
        hidden[held, :] = (gate_act * sigmoid_gate * up_act).astype(jnp.bfloat16)
        hidden_grads[held, pl.ds(0, hidden_width)] = (
            grads * up_act * sigmoid_gate * (1.0 + gate_act * (1.0 - sigmoid_gate))
        ).astype(jnp.bfloat16)
        hidden_grads[held, pl.ds(hidden_width, hidden_width)] = (
            grads * gate_act * sigmoid_gate
        ).astype(jnp.bfloat16)

    def second_half(low, high, piece):
        span = pl.ds(low, high - low)
        held = pl.ds(0, high - low)
        pieces = cent_all[span, pl.ds(width, 128)].astype(jnp.float32)
        lanes = lax.broadcasted_iota(jnp.int32, (high - low, 128), 1)
        own = (lanes % experts == me) & (lanes < 3 * experts)
        weight = jnp.sum(jnp.where(own, pieces, 0.0), axis=1, keepdims=True)
        columns = pl.ds(piece * wide, wide)
        output = jnp.dot(hidden[held, :], down[:, columns], preferred_element_type=jnp.float32)
        output = output.astype(jnp.bfloat16).astype(jnp.float32)
        part_cent[span, columns] = output * weight
        summed = jnp.dot(
            hidden_grads[held, :], gate_up_turned[:, columns], preferred_element_type=jnp.float32
        )
        summed = summed.astype(jnp.bfloat16).astype(jnp.float32)
        part_grad[span, columns] = summed * weight

    def contribution(kind, distance, piece):
        columns = pl.ds(piece * wide, wide)
        twin_copy(kind, distance, piece).wait_recv()
        return (
            parts[kind][block(distance, 0), columns]
            + twins[kind][pl.ds(places[distance] * rows, rows), columns]
        )

    def toward(way, distance):
        return distance if way == 0 else -distance

    def send_first(kind, way, piece):
        total = contribution(kind, toward(way, hops_of(kind, way)), piece)
        outgoing[kind, way, 0, piece] = total.astype(jnp.bfloat16)
        start(ring_copy(kind, way, 1, piece))

    def pass_on(hop, kind):
        for way in range(2):
            if hop <= hops_of(kind, way):
                gather_copy(kind, way, hop).wait_recv()
                if hop < hops_of(kind, way):
                    start(gather_copy(kind, way, hop + 1))
                start(share_copy(kind, signed(way, hop)))

    def distances_of(hop):
        if hop == 0 or hop == half:
            return (hop,)
        return (hop, -hop)

    def wait_shares(hop):
        for kind in range(2):
            for distance in distances_of(hop):
                share_copy(kind, distance).wait_recv()

    def start_twins(hop, piece):
        for distance in distances_of(hop):
            for kind in range(2):
                start(twin_copy(kind, distance, piece))

    bands = width // tile
    pass_on(1, 0)
    weight_copies[2].wait()
    turn(down, down_turned, 0, hidden_width // tile)
    pass_on(1, 1)
    weight_copies[0].wait()
    weight_copies[1].wait()
    turn(gate_up, gate_up_turned, 0, bands // 2)
    pass_on(2, 0)
    turn(gate_up, gate_up_turned, bands // 2, bands)
    pass_on(2, 1)
    low = 0
    for hop in range(1, half + 1):
        included = (0, 1) if hop == 1 else (hop,)
        high = low + sum(len(distances_of(each)) for each in included) * 2 * rows
        for each in included:
            wait_shares(each)
        first_half(low, high)
        if hop < half - 1:
            pass_on(hop + 2, 0)
        if hop == half:
            for kind in range(2):
                for piece in range(2):
                    send_first(kind, 1 - kind, piece)
        for piece in range(2):
            second_half(low, high, piece)
            for each in included:
                start_twins(each, piece)
        if hop < half - 1:
            pass_on(hop + 2, 1)
        low = high

    for piece in range(2):
        for kind in range(2):
            send_first(kind, kind, piece)
    deltas = (delta_ref, delta_grad_ref)
    keeps = (centroid_keep, grad_keep)
    for kind in range(2):
        for piece in range(2):
            columns = pl.ds(piece * wide, wide)
            total = contribution(kind, 0, piece)
            deltas[kind][:, columns] = total - keeps[kind][:, columns]
    for step in range(1, half + 1):
        for piece in range(2):
            columns = pl.ds(piece * wide, wide)
            for kind in range(2):
                for way in (1 - kind, kind):
                    hops = hops_of(kind, way)
                    if step > hops:
                        continue
                    ring_copy(kind, way, step, piece).wait_recv()
                    arrived = incoming[kind, way, step - 1, piece].astype(jnp.float32)
                    if step < hops:
                        total = arrived + contribution(kind, toward(way, hops - step), piece)
                        outgoing[kind, way, step, piece] = total.astype(jnp.bfloat16)
                        start(ring_copy(kind, way, step + 1, piece))
                    else:
                        deltas[kind][:, columns] += arrived
    delta_grad_ref[...] = delta_grad_ref[...] / counts
    for copy in started:
        copy.wait_send()


def decode_kernel(ids_ref, tokens_ref, out_grad_ref, delta_ref, delta_grad_ref, out_ref, grad_ref):
    rows = delta_ref.shape[0]
    lines = lax.broadcasted_iota(jnp.int32, (3 * rows, ids_ref.shape[1]), 0)
    members = (lines % rows == ids_ref[...]).astype(jnp.bfloat16)
    contract = (((0,), (0,)), ((), ()))

    def spread(table):
        high = table.astype(jnp.bfloat16)
        rest = table - high.astype(jnp.float32)
        middle = rest.astype(jnp.bfloat16)
        low = (rest - middle.astype(jnp.float32)).astype(jnp.bfloat16)
        stacked = jnp.concatenate([high, middle, low], axis=0)
        return lax.dot_general(members, stacked, contract, preferred_element_type=jnp.float32)

    out_ref[...] = tokens_ref[...].astype(jnp.float32) + spread(delta_ref[...])
    grad_ref[...] = out_grad_ref[...].astype(jnp.float32) + spread(delta_grad_ref[...])


def ring_per_device(
    tokens, out_grad, cluster_ids, routes, route_weights, gate_weight, up_weight, down_weight
):
    experts = lax.axis_size("expert")
    rows = routes.shape[0]
    count, width = tokens.shape
    hidden_width = gate_weight.shape[2]
    ring = experts // 2
    half = ring // 2
    held = experts * rows
    ids = cluster_ids.reshape(1, count)
    vmem = pl.BlockSpec(memory_space=pltpu.VMEM)
    anywhere = pl.BlockSpec(memory_space=pl.ANY)
    table = jax.ShapeDtypeStruct((rows, width), jnp.float32)
    bf16, f32, dma = jnp.bfloat16, jnp.float32, pltpu.SemaphoreType.DMA
    delta, delta_grad = pl.pallas_call(
        functools.partial(exchange_kernel, experts),
        out_shape=(table, table),
        in_specs=[vmem] * 5 + [anywhere] * 3,
        out_specs=(vmem, vmem),
        scratch_shapes=[
            pltpu.VMEM((held, width + 128), bf16),
            pltpu.VMEM((held, width), bf16),
            pltpu.VMEM((width, 2 * hidden_width), bf16),
            pltpu.VMEM((hidden_width, width), bf16),
            pltpu.VMEM((2 * hidden_width, width), bf16),
            pltpu.VMEM((width, hidden_width), bf16),
            pltpu.VMEM((6 * rows, hidden_width), bf16),
            pltpu.VMEM((6 * rows, 2 * hidden_width), bf16),
            pltpu.VMEM((held, width), f32),
            pltpu.VMEM((held, width), f32),
            pltpu.VMEM((ring * rows, width), f32),
            pltpu.VMEM((ring * rows, width), f32),
            pltpu.VMEM((2, 2, half, 2, rows, width // 2), bf16),
            pltpu.VMEM((2, 2, half, 2, rows, width // 2), bf16),
            pltpu.VMEM((rows, width), f32),
            pltpu.VMEM((rows, width), f32),
            dma((3,)),
            dma((2, 2, half)),
            dma((2, 2, half)),
            dma((2, ring)),
            dma((2, ring)),
            dma((2, ring, 2)),
            dma((2, ring, 2)),
            dma((2, 2, half, 2)),
            dma((2, 2, half, 2)),
        ],
        compiler_params=pltpu.CompilerParams(
            collective_id=0, has_side_effects=True, vmem_limit_bytes=56 * 1024 * 1024
        ),
        cost_estimate=pl.CostEstimate(
            flops=12 * held * width * hidden_width,
            bytes_accessed=6 * width * hidden_width,
            transcendentals=held * hidden_width,
        ),
    )(ids, tokens, out_grad, routes.T, route_weights.T, gate_weight, up_weight, down_weight)
    result = jax.ShapeDtypeStruct((count, width), jnp.float32)
    return pl.pallas_call(
        decode_kernel,
        out_shape=(result, result),
        in_specs=[vmem] * 5,
        out_specs=(vmem, vmem),
    )(ids, tokens, out_grad, delta, delta_grad)


def solution(mesh):
    placed = (
        P(("groups", "expert"), None),
        P(("groups", "expert"), None),
        P(("groups", "expert")),
        P(("groups", "expert"), None),
        P(("groups", "expert"), None),
        P("expert", None, None),
        P("expert", None, None),
        P("expert", None, None),
    )
    size = mesh.shape["expert"]
    ringed = size % 4 == 0 and 12 <= size <= 32
    return jax.shard_map(
        ring_per_device if ringed else per_device,
        mesh=mesh,
        in_specs=placed,
        out_specs=(P(("groups", "expert"), None), P(("groups", "expert"), None)),
        check_vma=False,
    )
```

```python
import functools
import jax
import jax.numpy as jnp
from jax import lax
from jax.experimental import pallas as pl
from jax.experimental.pallas import tpu as pltpu
from jax.sharding import PartitionSpec as P


def expert_forward(inputs, gate_mat, up_mat, down_mat):
    gate_act = jnp.dot(inputs, gate_mat, preferred_element_type=jnp.float32)
    up_act = jnp.dot(inputs, up_mat, preferred_element_type=jnp.float32)
    sigmoid_gate = jax.nn.sigmoid(gate_act)
    hidden = (gate_act * sigmoid_gate * up_act).astype(jnp.bfloat16)
    output = jnp.dot(hidden, down_mat, preferred_element_type=jnp.float32).astype(jnp.bfloat16)
    return (output, gate_act, up_act)


def expert_backward(incoming, gate_act, up_act, gate_mat, up_mat, down_mat):
    against = (((1,), (1,)), ((), ()))
    hidden_grad = lax.dot_general(incoming, down_mat, against, preferred_element_type=jnp.float32)
    sigmoid_gate = jax.nn.sigmoid(gate_act)
    gate_grad = (
        hidden_grad * up_act * sigmoid_gate * (1.0 + gate_act * (1.0 - sigmoid_gate))
    ).astype(jnp.bfloat16)
    up_grad = (hidden_grad * gate_act * sigmoid_gate).astype(jnp.bfloat16)
    summed = lax.dot_general(gate_grad, gate_mat, against, preferred_element_type=jnp.float32)
    summed = summed + lax.dot_general(up_grad, up_mat, against, preferred_element_type=jnp.float32)
    return summed.astype(jnp.bfloat16)


def per_device(
    tokens, out_grad, cluster_ids, routes, route_weights, gate_weight, up_weight, down_weight
):
    model_width = tokens.shape[1]
    cent_rows = routes.shape[0]
    fanout = routes.shape[1]
    experts = lax.axis_size("expert")
    capacity = min(cent_rows, 2 * cent_rows * fanout // experts)
    member = (cluster_ids[:, None] == jnp.arange(cent_rows, dtype=jnp.int32)[None, :]).astype(
        jnp.bfloat16
    )
    counts = jnp.sum(member.astype(jnp.float32), axis=0)
    contract = (((0,), (0,)), ((), ()))
    centroid = (
        lax.dot_general(member, tokens, contract, preferred_element_type=jnp.float32)
        / counts[:, None]
    )
    grad_sum = lax.dot_general(member, out_grad, contract, preferred_element_type=jnp.float32)
    pair_ids = routes.reshape(-1)
    matches = (pair_ids[:, None] == jnp.arange(experts, dtype=jnp.int32)[None, :]).astype(jnp.int32)
    earlier = jnp.cumsum(matches, axis=0) - matches
    position = jnp.sum(earlier * matches, axis=1)
    slot_of = (pair_ids * capacity + position).reshape(cent_rows, fanout)
    slot_range = jnp.arange(experts * capacity, dtype=jnp.int32)
    placing = jnp.any(slot_of[None, :, :] == slot_range[:, None, None], axis=2).astype(jnp.bfloat16)
    send_cent = jnp.dot(placing, centroid.astype(jnp.bfloat16), preferred_element_type=jnp.float32)
    send_cent = send_cent.astype(jnp.bfloat16).reshape(experts, capacity, model_width)
    send_grad = jnp.dot(placing, grad_sum.astype(jnp.bfloat16), preferred_element_type=jnp.float32)
    send_grad = send_grad.astype(jnp.bfloat16).reshape(experts, capacity, model_width)
    gate_mat = gate_weight[0]
    up_mat = up_weight[0]
    down_mat = down_weight[0]
    arrived = lax.all_to_all(send_cent, "expert", split_axis=0, concat_axis=0, tiled=True)
    output, gate_act, up_act = expert_forward(
        arrived.reshape(-1, model_width), gate_mat, up_mat, down_mat
    )
    results = lax.all_to_all(
        output.reshape(experts, capacity, model_width),
        "expert",
        split_axis=0,
        concat_axis=0,
        tiled=True,
    )
    arrived_grad = lax.all_to_all(send_grad, "expert", split_axis=0, concat_axis=0, tiled=True)
    input_grad = expert_backward(
        arrived_grad.reshape(-1, model_width), gate_act, up_act, gate_mat, up_mat, down_mat
    )
    results_grad = lax.all_to_all(
        input_grad.reshape(experts, capacity, model_width),
        "expert",
        split_axis=0,
        concat_axis=0,
        tiled=True,
    )
    returned = results.reshape(-1, model_width)[slot_of]
    returned_grad = results_grad.reshape(-1, model_width)[slot_of]
    combined = jnp.sum(route_weights[:, :, None] * returned.astype(jnp.float32), axis=1)
    centroid_grad = (
        jnp.sum(route_weights[:, :, None] * returned_grad.astype(jnp.float32), axis=1) - grad_sum
    )
    layer_out = tokens.astype(jnp.float32) + jnp.take(combined - centroid, cluster_ids, axis=0)
    token_grad = out_grad.astype(jnp.float32) + jnp.take(
        centroid_grad / counts[:, None], cluster_ids, axis=0
    )
    return (layer_out, token_grad)


AGAINST = (((1,), (1,)), ((), ()))


def ring_layout(ring):
    half = ring // 2
    places = {0: 0}
    for hop in range(1, half):
        places[hop] = 2 * hop - 1
        places[-hop] = 2 * hop
    places[half] = ring - 1
    places[-half] = ring - 1
    return places


def exchange_kernel(
    experts,
    ids_ref,
    tokens_ref,
    out_grad_ref,
    routes_ref,
    route_weights_ref,
    gate_ref,
    up_ref,
    down_ref,
    delta_ref,
    delta_grad_ref,
    cent_all,
    grad_all,
    gate_up,
    down,
    gate_up_turned,
    down_turned,
    hidden,
    hidden_grads,
    part_cent,
    part_grad,
    lend_cent,
    lend_grad,
    twin_cent,
    twin_grad,
    outgoing,
    incoming,
    centroid_keep,
    grad_keep,
    weight_sems,
    gather_send,
    gather_recv,
    share_send,
    share_recv,
    twin_send,
    twin_recv,
    ring_send,
    ring_recv,
):
    fanout, rows = routes_ref.shape
    width = tokens_ref.shape[1]
    hidden_width = down.shape[0]
    ring = experts // 2
    half = ring // 2
    wide = width // 2
    places = ring_layout(ring)
    gathered = (cent_all, grad_all)
    parts = (part_cent, part_grad)
    lends = (lend_cent, lend_grad)
    twins = (twin_cent, twin_grad)

    me = lax.axis_index("expert")
    core = me % 2
    chip = me // 2
    column = chip % 2
    height = chip // 2
    spot = height + column * (ring - 1 - 2 * height)

    def device_at(position):
        side = position // half
        level = position + side * (ring - 1 - 2 * position)
        return (level * 2 + side) * 2 + core

    neighbour = (device_at((spot + 1) % ring), device_at((spot + ring - 1) % ring))
    twin = chip * 2 + (1 - core)

    weight_copies = [
        pltpu.make_async_copy(
            gate_ref.at[0], gate_up.at[:, pl.ds(0, hidden_width)], weight_sems.at[0]
        ),
        pltpu.make_async_copy(
            up_ref.at[0], gate_up.at[:, pl.ds(hidden_width, hidden_width)], weight_sems.at[1]
        ),
        pltpu.make_async_copy(down_ref.at[0], down, weight_sems.at[2]),
    ]
    for number in (2, 0, 1):
        weight_copies[number].start()

    barrier = pltpu.get_barrier_semaphore()
    for other in (neighbour[0], neighbour[1], twin):
        pl.semaphore_signal(
            barrier, inc=1, device_id={"expert": other}, device_id_type=pl.DeviceIdType.MESH
        )

    def block(distance, which):
        return pl.ds((places[distance] * 2 + which) * rows, rows)

    members = (
        lax.broadcasted_iota(jnp.int32, (rows, ids_ref.shape[1]), 0) == ids_ref[...]
    ).astype(jnp.float32)
    counts = jnp.sum(members, axis=1, keepdims=True)
    members = members.astype(jnp.bfloat16)
    centroid = jnp.dot(members, tokens_ref[...], preferred_element_type=jnp.float32) / counts
    grad_sum = jnp.dot(members, out_grad_ref[...], preferred_element_type=jnp.float32)
    centroid_keep[...] = centroid
    grad_keep[...] = grad_sum
    cent_all[block(0, 0), pl.ds(0, width)] = centroid.astype(jnp.bfloat16)
    grad_all[block(0, 0), :] = grad_sum.astype(jnp.bfloat16)

    lanes = lax.broadcasted_iota(jnp.int32, (128, rows), 0)
    spread = jnp.zeros((128, rows), jnp.float32)
    for k in range(fanout):
        spread = spread + jnp.where(
            lanes % experts == routes_ref[k : k + 1, :], route_weights_ref[k : k + 1, :], 0.0
        )
    high = spread.astype(jnp.bfloat16).astype(jnp.float32)
    middle = (spread - high).astype(jnp.bfloat16).astype(jnp.float32)
    low = spread - high - middle
    pieces = jnp.where(lanes < experts, high, jnp.where(lanes < 2 * experts, middle, low))
    same = lax.broadcasted_iota(jnp.int32, (rows, rows), 0) == lax.broadcasted_iota(
        jnp.int32, (rows, rows), 1
    )
    pieces = lax.dot_general(
        same.astype(jnp.bfloat16),
        pieces.astype(jnp.bfloat16),
        AGAINST,
        preferred_element_type=jnp.float32,
    )
    cent_all[block(0, 0), pl.ds(width, 128)] = pieces.astype(jnp.bfloat16)

    def remote(source, target, send, recv, other):
        return pltpu.make_async_remote_copy(
            src_ref=source,
            dst_ref=target,
            send_sem=send,
            recv_sem=recv,
            device_id={"expert": other},
            device_id_type=pl.DeviceIdType.MESH,
        )

    def signed(way, distance):
        return -distance if way == 0 else distance

    def hops_of(kind, way):
        return half if kind == way else half - 1

    def gather_copy(kind, way, hop):
        return remote(
            gathered[kind].at[block(signed(way, hop - 1), 0), :],
            gathered[kind].at[block(signed(way, hop), 0), :],
            gather_send.at[kind, way, hop - 1],
            gather_recv.at[kind, way, hop - 1],
            neighbour[way],
        )

    def share_copy(kind, distance):
        return remote(
            gathered[kind].at[block(distance, 0), :],
            gathered[kind].at[block(distance, 1), :],
            share_send.at[kind, places[distance]],
            share_recv.at[kind, places[distance]],
            twin,
        )

    def twin_copy(kind, distance, piece):
        columns = pl.ds(piece * wide, wide)
        return remote(
            lends[kind].at[pl.ds(places[distance] * rows, rows), columns],
            twins[kind].at[pl.ds(places[distance] * rows, rows), columns],
            twin_send.at[kind, places[distance], piece],
            twin_recv.at[kind, places[distance], piece],
            twin,
        )

    def ring_copy(kind, way, step, piece):
        return remote(
            outgoing.at[kind, way, step - 1, piece],
            incoming.at[kind, way, step - 1, piece],
            ring_send.at[kind, way, step - 1, piece],
            ring_recv.at[kind, way, step - 1, piece],
            neighbour[way],
        )

    started = []

    def start(copy):
        copy.start()
        started.append(copy)

    pl.semaphore_wait(barrier, 3)
    for way in range(2):
        for kind in range(2):
            start(gather_copy(kind, way, 1))
    for kind in range(2):
        start(share_copy(kind, 0))

    tile = 256 if hidden_width % 256 == 0 else hidden_width

    def turn(source, target, first, last):
        across = source.shape[1] // tile

        def body(r, carry):
            lines = pl.ds(pl.multiple_of(r * tile, tile), tile)
            for c in range(across):
                columns = pl.ds(c * tile, tile)
                target[columns, lines] = source[lines, columns].T
            return carry

        lax.fori_loop(first, last, body, 0)

    def first_half(low, high):
        span = pl.ds(low, high - low)
        held = pl.ds(0, high - low)

        acts = jnp.dot(
            cent_all[span, pl.ds(0, width)], gate_up[...], preferred_element_type=jnp.float32
        )
        grads = jnp.dot(grad_all[span, :], down_turned[...], preferred_element_type=jnp.float32)
        gate_act = acts[:, :hidden_width]
        up_act = acts[:, hidden_width:]
        sigmoid_gate = jax.nn.sigmoid(gate_act)
        hidden[held, :] = (gate_act * sigmoid_gate * up_act).astype(jnp.bfloat16)
        hidden_grads[held, pl.ds(0, hidden_width)] = (
            grads * up_act * sigmoid_gate * (1.0 + gate_act * (1.0 - sigmoid_gate))
        ).astype(jnp.bfloat16)
        hidden_grads[held, pl.ds(hidden_width, hidden_width)] = (
            grads * gate_act * sigmoid_gate
        ).astype(jnp.bfloat16)

    def keep(kind, low, columns, values):
        for number in range(values.shape[0] // (2 * rows)):
            lines = pl.ds(low // 2 + number * rows, rows)
            first = 2 * number * rows
            parts[kind][lines, columns] = values[first : first + rows]
            lends[kind][lines, columns] = values[first + rows : first + 2 * rows].astype(
                jnp.bfloat16
            )

    def second_half(low, high, piece):
        span = pl.ds(low, high - low)
        held = pl.ds(0, high - low)
        pieces = cent_all[span, pl.ds(width, 128)].astype(jnp.float32)
        lanes = lax.broadcasted_iota(jnp.int32, (high - low, 128), 1)
        own = (lanes % experts == me) & (lanes < 3 * experts)
        weight = jnp.sum(jnp.where(own, pieces, 0.0), axis=1, keepdims=True)
        columns = pl.ds(piece * wide, wide)
        output = jnp.dot(hidden[held, :], down[:, columns], preferred_element_type=jnp.float32)
        output = output.astype(jnp.bfloat16).astype(jnp.float32)
        keep(0, low, columns, output * weight)
        summed = jnp.dot(
            hidden_grads[held, :], gate_up_turned[:, columns], preferred_element_type=jnp.float32
        )
        summed = summed.astype(jnp.bfloat16).astype(jnp.float32)
        keep(1, low, columns, summed * weight)

    def contribution(kind, distance, piece):
        columns = pl.ds(piece * wide, wide)
        twin_copy(kind, distance, piece).wait_recv()
        return (
            parts[kind][pl.ds(places[distance] * rows, rows), columns]
            + twins[kind][pl.ds(places[distance] * rows, rows), columns].astype(jnp.float32)
        )

    def toward(way, distance):
        return distance if way == 0 else -distance

    def send_first(kind, way, piece):
        total = contribution(kind, toward(way, hops_of(kind, way)), piece)
        outgoing[kind, way, 0, piece] = total.astype(jnp.bfloat16)
        start(ring_copy(kind, way, 1, piece))

    def pass_on(hop, kind):
        for way in range(2):
            if hop <= hops_of(kind, way):
                gather_copy(kind, way, hop).wait_recv()
                if hop < hops_of(kind, way):
                    start(gather_copy(kind, way, hop + 1))
                start(share_copy(kind, signed(way, hop)))

    def distances_of(hop):
        if hop == 0 or hop == half:
            return (hop,)
        return (hop, -hop)

    def wait_shares(hop):
        for kind in range(2):
            for distance in distances_of(hop):
                share_copy(kind, distance).wait_recv()

    def start_twins(hop, piece):
        for distance in distances_of(hop):
            for kind in range(2):
                start(twin_copy(kind, distance, piece))

    bands = width // tile
    pass_on(1, 0)
    weight_copies[2].wait()
    turn(down, down_turned, 0, hidden_width // tile)
    pass_on(1, 1)
    weight_copies[0].wait()
    weight_copies[1].wait()
    turn(gate_up, gate_up_turned, 0, bands // 2)
    pass_on(2, 0)
    turn(gate_up, gate_up_turned, bands // 2, bands)
    pass_on(2, 1)
    low = 0
    for hop in range(1, half + 1):
        included = (0, 1) if hop == 1 else (hop,)
        high = low + sum(len(distances_of(each)) for each in included) * 2 * rows
        for each in included:
            wait_shares(each)
        first_half(low, high)
        if hop < half - 1:
            pass_on(hop + 2, 0)
        if hop == half:
            for kind in range(2):
                for piece in range(2):
                    send_first(kind, 1 - kind, piece)
        for piece in range(2):
            second_half(low, high, piece)
            for each in included:
                start_twins(each, piece)
        if hop < half - 1:
            pass_on(hop + 2, 1)
        low = high

    for piece in range(2):
        for kind in range(2):
            send_first(kind, kind, piece)
    deltas = (delta_ref, delta_grad_ref)
    keeps = (centroid_keep, grad_keep)
    for kind in range(2):
        for piece in range(2):
            columns = pl.ds(piece * wide, wide)
            total = contribution(kind, 0, piece)
            deltas[kind][:, columns] = total - keeps[kind][:, columns]
    for step in range(1, half + 1):
        for piece in range(2):
            columns = pl.ds(piece * wide, wide)
            for kind in range(2):
                for way in (1 - kind, kind):
                    hops = hops_of(kind, way)
                    if step > hops:
                        continue
                    ring_copy(kind, way, step, piece).wait_recv()
                    arrived = incoming[kind, way, step - 1, piece].astype(jnp.float32)
                    if step < hops:
                        total = arrived + contribution(kind, toward(way, hops - step), piece)
                        outgoing[kind, way, step, piece] = total.astype(jnp.bfloat16)
                        start(ring_copy(kind, way, step + 1, piece))
                    else:
                        deltas[kind][:, columns] += arrived
    delta_grad_ref[...] = delta_grad_ref[...] / counts
    for copy in started:
        copy.wait_send()


def decode_kernel(ids_ref, tokens_ref, out_grad_ref, delta_ref, delta_grad_ref, out_ref, grad_ref):
    rows = delta_ref.shape[0]
    lines = lax.broadcasted_iota(jnp.int32, (3 * rows, ids_ref.shape[1]), 0)
    members = (lines % rows == ids_ref[...]).astype(jnp.bfloat16)
    contract = (((0,), (0,)), ((), ()))

    def spread(table):
        high = table.astype(jnp.bfloat16)
        rest = table - high.astype(jnp.float32)
        middle = rest.astype(jnp.bfloat16)
        low = (rest - middle.astype(jnp.float32)).astype(jnp.bfloat16)
        stacked = jnp.concatenate([high, middle, low], axis=0)
        return lax.dot_general(members, stacked, contract, preferred_element_type=jnp.float32)

    out_ref[...] = tokens_ref[...].astype(jnp.float32) + spread(delta_ref[...])
    grad_ref[...] = out_grad_ref[...].astype(jnp.float32) + spread(delta_grad_ref[...])


def ring_per_device(
    tokens, out_grad, cluster_ids, routes, route_weights, gate_weight, up_weight, down_weight
):
    experts = lax.axis_size("expert")
    rows = routes.shape[0]
    count, width = tokens.shape
    hidden_width = gate_weight.shape[2]
    ring = experts // 2
    half = ring // 2
    held = experts * rows
    ids = cluster_ids.reshape(1, count)
    vmem = pl.BlockSpec(memory_space=pltpu.VMEM)
    anywhere = pl.BlockSpec(memory_space=pl.ANY)
    table = jax.ShapeDtypeStruct((rows, width), jnp.float32)
    bf16, f32, dma = jnp.bfloat16, jnp.float32, pltpu.SemaphoreType.DMA
    delta, delta_grad = pl.pallas_call(
        functools.partial(exchange_kernel, experts),
        out_shape=(table, table),
        in_specs=[vmem] * 5 + [anywhere] * 3,
        out_specs=(vmem, vmem),
        scratch_shapes=[
            pltpu.VMEM((held, width + 128), bf16),
            pltpu.VMEM((held, width), bf16),
            pltpu.VMEM((width, 2 * hidden_width), bf16),
            pltpu.VMEM((hidden_width, width), bf16),
            pltpu.VMEM((2 * hidden_width, width), bf16),
            pltpu.VMEM((width, hidden_width), bf16),
            pltpu.VMEM((6 * rows, hidden_width), bf16),
            pltpu.VMEM((6 * rows, 2 * hidden_width), bf16),
            pltpu.VMEM((ring * rows, width), f32),
            pltpu.VMEM((ring * rows, width), f32),
            pltpu.VMEM((ring * rows, width), bf16),
            pltpu.VMEM((ring * rows, width), bf16),
            pltpu.VMEM((ring * rows, width), bf16),
            pltpu.VMEM((ring * rows, width), bf16),
            pltpu.VMEM((2, 2, half, 2, rows, width // 2), bf16),
            pltpu.VMEM((2, 2, half, 2, rows, width // 2), bf16),
            pltpu.VMEM((rows, width), f32),
            pltpu.VMEM((rows, width), f32),
            dma((3,)),
            dma((2, 2, half)),
            dma((2, 2, half)),
            dma((2, ring)),
            dma((2, ring)),
            dma((2, ring, 2)),
            dma((2, ring, 2)),
            dma((2, 2, half, 2)),
            dma((2, 2, half, 2)),
        ],
        compiler_params=pltpu.CompilerParams(
            collective_id=0, has_side_effects=True, vmem_limit_bytes=56 * 1024 * 1024
        ),
        cost_estimate=pl.CostEstimate(
            flops=12 * held * width * hidden_width,
            bytes_accessed=6 * width * hidden_width,
            transcendentals=held * hidden_width,
        ),
    )(ids, tokens, out_grad, routes.T, route_weights.T, gate_weight, up_weight, down_weight)
    result = jax.ShapeDtypeStruct((count, width), jnp.float32)
    return pl.pallas_call(
        decode_kernel,
        out_shape=(result, result),
        in_specs=[vmem] * 5,
        out_specs=(vmem, vmem),
    )(ids, tokens, out_grad, delta, delta_grad)


def solution(mesh):
    placed = (
        P(("groups", "expert"), None),
        P(("groups", "expert"), None),
        P(("groups", "expert")),
        P(("groups", "expert"), None),
        P(("groups", "expert"), None),
        P("expert", None, None),
        P("expert", None, None),
        P("expert", None, None),
    )
    size = mesh.shape["expert"]
    ringed = size % 4 == 0 and 12 <= size <= 32
    return jax.shard_map(
        ring_per_device if ringed else per_device,
        mesh=mesh,
        in_specs=placed,
        out_specs=(P(("groups", "expert"), None), P(("groups", "expert"), None)),
        check_vma=False,
    )
```
